32 devices in a mesh: row: 4 (over x, core), col: 8 (over z, y).
Axes of the slice: x: 2, y: 2, z: 4, core: 2. Of those that a mesh axis runs over, the one named last changes fastest.
Arguments:
- tile_feats: bfloat16 [32, 32, 128, 192], P(('row', 'col')), may hold values from -6 to 6
- tile_cell: int32 [32, 32, 128], P(('row', 'col')), may hold values from 0 to 4095, as said below
- tile_mask: int32 [32, 32, 128], P(('row', 'col')), may hold values 0 or 1
- tile_count: int32 [32, 32], P(('row', 'col')), may hold values from 0 to 128, as said below
- background: bfloat16 [192], replicated, may hold values from -6 to 6
- norm_gain: float32 [192], replicated, may hold values from 0.1 to 1.9
- in_x: bfloat16 [192, 384], replicated, may hold values from -0.4375 to 0.4375
- in_z: bfloat16 [192, 384], replicated, may hold values from -0.4375 to 0.4375
- conv_w: float32 [3, 3, 384], replicated, may hold values from -2 to 2
- conv_bias: float32 [384], replicated, may hold values from -3 to 3
- x_proj: bfloat16 [384, 128], replicated, may hold values from -0.15625 to 0.15625
- skip_gain: float32 [384], replicated, may hold values from 0.5 to 1.5
- decay_rate: float32 [4, 6, 128, 1024], P(None, None, 'row', 'col'), may hold values from 0 to 1
- out_gain: float32 [384], replicated, may hold values from 0.1 to 1.9
- out_w: bfloat16 [384, 192], replicated, may hold values from -0.3125 to 0.3125
- mlp_gain: float32 [192], replicated, may hold values from 0.1 to 1.9
- ff_in: bfloat16 [192, 768], replicated, may hold values from -0.4375 to 0.4375
- ff_out: bfloat16 [768, 192], replicated, may hold values from -0.21875 to 0.21875
Outputs:
- block_out: bfloat16 [128, 1024, 192], P('row', 'col')
The draws below stay inside these ranges and needn't reach their ends.
Inputs may be any that keep to these rules, and one draw needn't show every extreme that they name: `tile_cell`: cells of the owner's block of 32 x 128 cells, numbered row by row; the live slots sent to one owner by all loaders name distinct cells. `tile_count`: the live slots from a loader to an owner are its first ones; some owner receives 128 from every loader.
All inputs are finite; a program needn't handle non-finite values. No bound on the sum of `tile_mask` on one device may be relied on, other than what follows from the above.
Results may differ from the reference program's by a relative error of at most 0.015.
Values may be sent and summed in bfloat16 or wider, within the bound.
A program may use at most 384 MiB of HBM per device.

```python
import math
import jax
import jax.numpy as jnp
from jax import lax

C = 192
DI = 384
STATE = 16
FF = 768
DIRS = 4
RH = 32
RW = 128
HEADS = 6
GRID_H = 128
GRID_W = 1024
CAP = 128
DEVICES = 32


def routing_parts(key):
    key_ceiling, key_count, key_full, key_order, key_filler = jax.random.split(jax.random.fold_in(key, 7), 5)
    ceiling = jax.random.randint(key_ceiling, (1, DEVICES), CAP // 2, CAP + 1)
    ceiling = jnp.broadcast_to(ceiling, (DEVICES, DEVICES))
    counts = jax.random.randint(key_count, (DEVICES, DEVICES), ceiling // 2, ceiling + 1)
    full_owner = jax.random.randint(key_full, (), 0, DEVICES)
    counts = jnp.where(jnp.arange(DEVICES)[None, :] == full_owner, CAP, counts)
    cells = RH * RW
    orders = jax.vmap(lambda subkey: jax.random.permutation(subkey, cells))(jax.random.split(key_order, DEVICES))
    offsets = jnp.cumsum(counts, axis=0) - counts
    slot_index = jnp.arange(CAP)
    position = jnp.minimum(offsets[:, :, None] + slot_index[None, None, :], cells - 1)
    picked = orders[jnp.arange(DEVICES)[None, :, None], position]
    filler = jax.random.randint(key_filler, (DEVICES, DEVICES, CAP), 0, cells)
    cell_ids = jnp.where(slot_index[None, None, :] < counts[:, :, None], picked, filler)
    return (counts.astype(jnp.int32), cell_ids.astype(jnp.int32))


def draw_tile_cell(key, part):
    return routing_parts(key)[1]


def draw_tile_count(key, part):
    return routing_parts(key)[0]


def draw_decay_rate(key, part):
    keys = jax.random.split(jax.random.fold_in(key, 11), 7)
    fast_share = 0.5
    fast = jax.random.uniform(keys[0], (DIRS, HEADS, 1, 1)) < fast_share
    chain = jnp.array([GRID_W, GRID_W, GRID_H, GRID_H], jnp.float32).reshape(DIRS, 1, 1, 1)
    fast_rate = jnp.exp(jax.random.uniform(keys[1], (DIRS, HEADS, 1, 1), minval=math.log(1.0 / 50.0), maxval=math.log(1.0 / 30.0)))
    slow_rate = jnp.exp(jax.random.uniform(keys[2], (DIRS, HEADS, 1, 1), minval=math.log(0.05), maxval=math.log(0.25))) / chain
    base = jnp.where(fast, fast_rate, slow_rate)
    factor = 2.0 ** jax.random.uniform(keys[3], (DIRS, HEADS, GRID_H // RH, GRID_W // RW), minval=-1.0, maxval=1.0)
    factor = jnp.repeat(jnp.repeat(factor, RH, axis=2), RW, axis=3)
    rough = jnp.clip(1.0 + 0.25 * jax.random.normal(keys[4], (DIRS, HEADS, GRID_H, GRID_W)), 0.5, 1.5)
    hit = jax.random.uniform(keys[5], (DIRS, HEADS, GRID_H, GRID_W)) < 2.0 / chain
    loss = jax.random.uniform(keys[6], (DIRS, HEADS, GRID_H, GRID_W), minval=0.22, maxval=0.69)
    rate = base * factor * rough + jnp.where(hit, loss, 0.0)
    return rate.astype(jnp.float32)


def set_ends(entries, own_key, smallest, high):
    longest = entries.shape.index(max(entries.shape))
    spots = []
    for shift in (0, 1):
        where = [jax.random.randint(jax.random.fold_in(own_key, axis), (), 0, length) for axis, length in enumerate(entries.shape)]
        where[longest] = (where[longest] + shift) % entries.shape[longest]
        spots.append(tuple(where))
    return entries.at[spots[0]].set(smallest).at[spots[1]].set(high)


def block_scale(stream_key, dims, cuts, least, top_value):
    def one(dim, parts):
        draws = jax.random.uniform(jax.random.fold_in(jax.random.fold_in(stream_key, 6), dim), (parts,), jnp.float32, least / len(cuts), top_value / len(cuts))
        return jnp.repeat(jnp.exp(draws), dims[dim] // parts).reshape((-1,) + (1,) * (len(dims) - dim - 1))

    factor_of = one(*cuts[0])
    for cut in cuts[1:]:
        factor_of = factor_of * one(*cut)
    return factor_of


def gaussian(stream_key, shape, scale, most, shards=(), held_as=jnp.bfloat16):
    values = jax.random.normal(stream_key, shape, jnp.float32) * scale
    if len(shards) > 0:
        values = block_scale(stream_key, shape, shards, -0.22, 0.18) * values
    return jnp.clip(values, min=-most, max=most).astype(held_as)


def setup_inputs(seed: int = 0) -> dict:
    key_of = jax.random.split(jax.random.key(seed), 19)
    tile_feats = gaussian(key_of[0], (DEVICES, DEVICES, CAP, C), 1.0, 6.0, ((0, 32),))
    tile_cell = draw_tile_cell(jax.random.fold_in(key_of[18], 71), 0)
    tile_mask = set_ends((jax.random.randint(key_of[2], (DEVICES, DEVICES, CAP), 0, 4) < 3).astype(jnp.int32), jax.random.fold_in(key_of[2], 1), 0, 1)
    tile_count = draw_tile_count(jax.random.fold_in(key_of[18], 71), 0)
    background = gaussian(key_of[4], (C,), 1.0, 6.0)
    norm_gain = jnp.clip(1.0 + 0.18 * jax.random.normal(key_of[5], (C,), jnp.float32), 0.1, 1.9)
    in_x = gaussian(key_of[6], (C, DI), C ** -0.5, 0.4375)
    in_z = gaussian(key_of[7], (C, DI), C ** -0.5, 0.4375)
    conv_w = gaussian(key_of[8], (3, 3, DI), 9 ** -0.5, 2.0, (), jnp.float32)
    conv_bias = gaussian(key_of[9], (DI,), 0.5, 3.0, (), jnp.float32)
    x_proj = gaussian(key_of[10], (DI, 2 * DIRS * STATE), (4 * DI) ** -0.5, 0.15625)
    skip_gain = jnp.clip(jax.random.uniform(key_of[11], (DI,), jnp.float32, 0.5, 1.5), 0.5, 1.5)
    decay_rate = draw_decay_rate(jax.random.fold_in(key_of[18], 71), 0)
    out_gain = jnp.clip(1.0 + 0.18 * jax.random.normal(key_of[13], (DI,), jnp.float32), 0.1, 1.9)
    out_w = gaussian(key_of[14], (DI, C), DI ** -0.5, 0.3125)
    mlp_gain = jnp.clip(1.0 + 0.18 * jax.random.normal(key_of[15], (C,), jnp.float32), 0.1, 1.9)
    ff_in = gaussian(key_of[16], (C, FF), C ** -0.5, 0.4375)
    ff_out = gaussian(key_of[17], (FF, C), FF ** -0.5, 0.21875)
    return dict(tile_feats=tile_feats, tile_cell=tile_cell, tile_mask=tile_mask, tile_count=tile_count, background=background, norm_gain=norm_gain, in_x=in_x, in_z=in_z, conv_w=conv_w, conv_bias=conv_bias, x_proj=x_proj, skip_gain=skip_gain, decay_rate=decay_rate, out_gain=out_gain, out_w=out_w, mlp_gain=mlp_gain, ff_in=ff_in, ff_out=ff_out)


def rms_scale(values, gains):
    return values * lax.rsqrt(lax.optimization_barrier(jnp.mean(values * values, axis=-1, keepdims=True)) + 1e-06) * gains

def block_parts(x_vals, b_coef, c_coef, rates):
    cumulative = jnp.cumsum(rates, axis=2)
    weight = jnp.sqrt(-jnp.expm1(-2.0 * rates))
    scaled = x_vals.astype(jnp.float32) * jnp.swapaxes(weight, 1, 2)[..., None]
    scores = jnp.einsum('stn,sun->stu', c_coef.astype(jnp.float32), b_coef.astype(jnp.float32))
    length = rates.shape[2]
    causal = lax.broadcasted_iota(jnp.int32, (length, length), 0) >= lax.broadcasted_iota(jnp.int32, (length, length), 1)
    log_gap = cumulative[:, :, :, None] - cumulative[:, :, None, :]
    mixing = jnp.where(causal, jnp.exp(-jnp.maximum(log_gap, 0.0)), 0.0) * scores[:, None]
    inner_part = jnp.einsum('shtu,suhp->sthp', mixing, scaled, precision=lax.Precision.HIGHEST)
    to_end = jnp.exp(cumulative - cumulative[:, :, -1:])
    weighted = scaled * jnp.swapaxes(to_end, 1, 2)[..., None]
    final_state = jnp.einsum('suhp,sun->shpn', weighted, b_coef.astype(jnp.float32), precision=lax.Precision.HIGHEST)
    total_decay = jnp.exp(-cumulative[:, :, -1])
    return (inner_part, final_state, total_decay, cumulative)

def carry_part(c_coef, cumulative, entering):
    reached = jnp.einsum('stn,shpn->sthp', c_coef.astype(jnp.float32), entering, precision=lax.Precision.HIGHEST)
    return reached * jnp.swapaxes(jnp.exp(-cumulative), 1, 2)[..., None]

def along_sequences(x_vals, b_coef, c_coef, rates, length):
    sequences, full_len, head_count, head_dim = x_vals.shape
    state_size = b_coef.shape[2]
    spans = full_len // length
    inputs = (jnp.moveaxis(x_vals.reshape(sequences, spans, length, head_count, head_dim), 1, 0), jnp.moveaxis(b_coef.reshape(sequences, spans, length, state_size), 1, 0), jnp.moveaxis(c_coef.reshape(sequences, spans, length, state_size), 1, 0), jnp.moveaxis(rates.reshape(sequences, head_count, spans, length), 2, 0))

    def advance(carried, block_args):
        inner_part, final_state, total_decay, cumulative = block_parts(*block_args)
        result = inner_part + carry_part(block_args[2], cumulative, carried)
        return (total_decay[:, :, None, None] * carried + final_state, result)
    initial = jnp.zeros((sequences, head_count, head_dim, state_size), jnp.float32)
    _, results = lax.scan(advance, initial, inputs)
    return jnp.moveaxis(results, 0, 1).reshape(sequences, full_len, head_count, head_dim)

def orient(direction, scan_in, coeffs, rate_all):
    rows_n, cols_n, width = scan_in.shape
    head_count = rate_all.shape[1]
    state_size = coeffs.shape[2] // 8
    x_vals = scan_in.reshape(rows_n, cols_n, head_count, width // head_count)
    b_coef = coeffs[:, :, 2 * direction * state_size:(2 * direction + 1) * state_size]
    c_coef = coeffs[:, :, (2 * direction + 1) * state_size:(2 * direction + 2) * state_size]
    rates = rate_all[direction]
    if direction >= 2:
        x_vals = jnp.swapaxes(x_vals, 0, 1)
        b_coef = jnp.swapaxes(b_coef, 0, 1)
        c_coef = jnp.swapaxes(c_coef, 0, 1)
        rates = jnp.transpose(rates, (2, 0, 1))
    else:
        rates = jnp.transpose(rates, (1, 0, 2))
    if direction % 2 == 1:
        x_vals = jnp.flip(x_vals, 1)
        b_coef = jnp.flip(b_coef, 1)
        c_coef = jnp.flip(c_coef, 1)
        rates = jnp.flip(rates, 2)
    return (x_vals, b_coef, c_coef, rates)

def restore(direction, result, rows_n, cols_n):
    if direction % 2 == 1:
        result = jnp.flip(result, 1)
    if direction >= 2:
        result = jnp.swapaxes(result, 0, 1)
    return result.reshape(rows_n, cols_n, -1)

def reference(tile_feats, tile_cell, tile_mask, tile_count, background, norm_gain, in_x, in_z, conv_w, conv_bias, x_proj, skip_gain, decay_rate, out_gain, out_w, mlp_gain, ff_in, ff_out):
    cols_dev = GRID_W // RW
    slot_live = jnp.arange(CAP, dtype=jnp.int32)[None, None, :] < tile_count[:, :, None]
    owner_index = jnp.arange(DEVICES, dtype=jnp.int32)[None, :, None]
    row_pos = owner_index // cols_dev * RH + tile_cell // RW
    col_pos = owner_index % cols_dev * RW + tile_cell % RW
    target = jnp.where(slot_live, row_pos * GRID_W + col_pos, GRID_H * GRID_W).astype(jnp.int32)
    values = jnp.where(tile_mask[..., None] == 1, tile_feats, background[None, None, None, :])
    tile_grid = jnp.zeros((GRID_H * GRID_W + 1, C), jnp.bfloat16).at[target.reshape(-1)].set(values.reshape(-1, C))
    tile_grid = tile_grid[:-1].reshape(GRID_H, GRID_W, C)

    def project(window):
        normed = rms_scale(window.astype(jnp.float32), norm_gain).astype(jnp.bfloat16)
        inner_x = jnp.dot(normed, in_x, preferred_element_type=jnp.float32).astype(jnp.bfloat16)
        gate_out = jnp.dot(normed, in_z, preferred_element_type=jnp.float32).astype(jnp.bfloat16)
        return (inner_x, gate_out)
    inner_x, gate_out = lax.map(project, tile_grid.reshape(GRID_H // RH, RH, GRID_W, C))
    inner_x = inner_x.reshape(GRID_H, GRID_W, DI)
    gate_out = gate_out.reshape(GRID_H, GRID_W, DI)
    padded = jnp.pad(inner_x, ((1, 1), (1, 1), (0, 0)))

    def convolve(block_index):
        window = lax.dynamic_slice_in_dim(padded, (block_index * RH).astype(jnp.int32), RH + 2, 0)
        summed_conv = jnp.zeros((RH, GRID_W, DI), jnp.float32) + conv_bias
        for shift_row in range(3):
            for shift_col in range(3):
                summed_conv = summed_conv + window[shift_row:shift_row + RH, shift_col:shift_col + GRID_W].astype(jnp.float32) * conv_w[shift_row, shift_col]
        return jax.nn.silu(summed_conv).astype(jnp.bfloat16)
    scan_in = lax.map(convolve, jnp.arange(GRID_H // RH, dtype=jnp.int32)).reshape(GRID_H, GRID_W, DI)
    coeffs = jnp.dot(scan_in, x_proj, preferred_element_type=jnp.float32).astype(jnp.bfloat16)
    summed = skip_gain * scan_in.astype(jnp.float32)
    for direction in range(DIRS):
        x_vals, b_coef, c_coef, rates = orient(direction, scan_in, coeffs, decay_rate)
        length = RH if direction >= 2 else RW
        result = along_sequences(x_vals, b_coef, c_coef, rates, length)
        summed = summed + restore(direction, result, GRID_H, GRID_W)

    def finish(window):
        summed_part, gate_part, grid_part = window
        gated_out = (rms_scale(summed_part, out_gain) * jax.nn.silu(gate_part.astype(jnp.float32))).astype(jnp.bfloat16)
        middle = (jnp.dot(gated_out, out_w, preferred_element_type=jnp.float32) + grid_part.astype(jnp.float32)).astype(jnp.bfloat16)
        normed_mid = rms_scale(middle.astype(jnp.float32), mlp_gain).astype(jnp.bfloat16)
        hidden = jax.nn.gelu(jnp.dot(normed_mid, ff_in, preferred_element_type=jnp.float32), approximate=False).astype(jnp.bfloat16)
        return (jnp.dot(hidden, ff_out, preferred_element_type=jnp.float32) + middle.astype(jnp.float32)).astype(jnp.bfloat16)
    blocks = GRID_H // RH
    block_out = lax.map(finish, (summed.reshape(blocks, RH, GRID_W, DI), gate_out.reshape(blocks, RH, GRID_W, DI), tile_grid.reshape(blocks, RH, GRID_W, C)))
    return block_out.reshape(GRID_H, GRID_W, C)
```

```python
import functools

import jax
import jax.numpy as jnp
from jax import lax
from jax.experimental import pallas as pl
from jax.experimental.pallas import tpu as pltpu
from jax.sharding import PartitionSpec as P

BF = jnp.bfloat16
F32 = jnp.float32
VMEM = pl.BlockSpec(memory_space=pltpu.VMEM)
PARAMS = dict(vmem_limit_bytes=56 * 1024 * 1024)
GROUP = 8
LANES = 128


def dot(a, b):
    return jnp.dot(a, b, preferred_element_type=F32)


def dot_t(a, b):
    return lax.dot_general(a, b, (((0,), (0,)), ((), ())), preferred_element_type=F32)


def silu(v):
    return v / (1.0 + jnp.exp(-v))


def rms(v, gains):
    return v * lax.rsqrt(jnp.mean(v * v, axis=-1, keepdims=True) + 1e-06) * gains


def place_kernel(cells_ref, values_ref, gain_ref, w_ref, grid_ref, x_ref, z_ref):
    tile, channels = grid_ref.shape
    slots = values_ref.shape[0]
    chunk = min(slots, 1024)
    base = pl.program_id(0) * tile
    ids = base + lax.broadcasted_iota(jnp.int32, (tile, chunk), 0)

    def add(k, acc):
        at = pl.ds(pl.multiple_of(k * chunk, chunk), chunk)
        hot = jnp.where(ids == cells_ref[:, at], 1.0, 0.0).astype(BF)
        return acc + dot(hot, values_ref[at, :])

    acc = lax.fori_loop(0, slots // chunk, add, jnp.zeros((tile, values_ref.shape[1]), F32))
    acc = acc[:, :channels]
    grid_ref[...] = acc.astype(BF)
    normed = rms(acc, gain_ref[...]).astype(BF)
    both = dot(normed, w_ref[...]).astype(BF)
    width = x_ref.shape[1]
    x_ref[...] = both[:, :width]
    z_ref[...] = both[:, width:]


def place(cells, values, gain, w, n_cells):
    channels, width = w.shape[0], w.shape[1] // 2
    tile = 512

    def whole(shape):
        return pl.BlockSpec(shape, lambda i: (0, 0))

    def rows(n):
        return pl.BlockSpec((tile, n), lambda i: (i, 0))

    return pl.pallas_call(
        place_kernel,
        grid=(n_cells // tile,),
        in_specs=[whole(cells.shape), whole(values.shape), whole(gain.shape), whole(w.shape)],
        out_specs=[rows(channels), rows(width), rows(width)],
        out_shape=[
            jax.ShapeDtypeStruct((n_cells, channels), BF),
            jax.ShapeDtypeStruct((n_cells, width), BF),
            jax.ShapeDtypeStruct((n_cells, width), BF),
        ],
        compiler_params=pltpu.CompilerParams(**PARAMS),
        name="place",
    )(cells, values, gain, w)


def lane_low(shape):
    return lax.broadcasted_iota(jnp.int32, shape, 1) < LANES // 2


def by_line(coef, lines):
    if lines == 1:
        return coef
    many = jnp.concatenate([coef] * lines, axis=0)
    line = lax.broadcasted_iota(jnp.int32, many.shape, 0) // coef.shape[0]
    own = lax.rem(lax.broadcasted_iota(jnp.int32, many.shape, 1), lines)
    return jnp.where(line == own, many, 0.0)


def coef_of(coefs, index, state):
    return coefs[index * state : (index + 1) * state, :].astype(F32)


def states(x, coefs, pair, vec, heads, state, lines, out_refs):
    for way in range(2):
        spread = by_line(coef_of(coefs, 2 * (2 * pair + way), state), lines)
        n = spread.shape[0]
        for p in range(heads // 2):
            both = jnp.concatenate(
                [spread * vec((3 + way) * heads + 2 * p + i) for i in range(2)], axis=0
            ).astype(BF)
            res = dot(both, x[:, p * LANES : (p + 1) * LANES])
            res = jnp.where(lane_low((n, LANES)), res[:n], res[n:])
            out_refs[way][:, p * LANES : (p + 1) * LANES] = res.astype(BF)


def inner(x, coefs, pair, vec, col, heads, state, lines):
    length = x.shape[0]
    shape = (length, length)
    t = lax.broadcasted_iota(jnp.int32, shape, 0)
    u = lax.broadcasted_iota(jnp.int32, shape, 1)
    ahead = t >= u
    same = t == u
    b0, c0, b1, c1 = (coefs[(4 * pair + i) * state : (4 * pair + i + 1) * state, :] for i in range(4))
    scores = jnp.where(ahead, dot_t(c0, b0), dot_t(c1, b1))
    if lines > 1:
        scores = jnp.where(lax.rem(t, lines) == lax.rem(u, lines), scores, 0.0)
    own = jnp.sum(b1.astype(F32) * c1.astype(F32), axis=0, keepdims=True)
    blocks = []
    for p in range(heads // 2):
        part = []
        for h in (2 * p, 2 * p + 1):
            gap = jnp.where(
                ahead,
                vec(h) - col[:, h : h + 1],
                vec(heads + h) - col[:, heads + h : heads + h + 1],
            )
            mix = jnp.exp(gap) * scores + jnp.where(same, vec(2 * heads + h) * own, 0.0)
            part.append(dot(mix.astype(BF), x[:, p * LANES : (p + 1) * LANES]))
        blocks.append(jnp.where(lane_low((length, LANES)), part[0], part[1]))
    return blocks


def entered(coefs, pair, vec, heads, state, lines, entering):
    spread = [by_line(coef_of(coefs, 2 * (2 * pair + way) + 1, state), lines) for way in range(2)]
    blocks = []
    for p in range(heads // 2):
        left, right = [], []
        for way in range(2):
            held = entering[way][:, p * LANES : (p + 1) * LANES].astype(F32)
            low = lane_low(held.shape)
            left += [spread[way] * vec((5 + way) * heads + 2 * p + i) for i in range(2)]
            right += [jnp.where(low, held, 0.0), jnp.where(low, 0.0, held)]
        blocks.append(
            dot_t(
                jnp.concatenate(left, axis=0).astype(BF), jnp.concatenate(right, axis=0).astype(BF)
            )
        )
    return blocks


def row_of(ref, g):
    return lambda i: ref[g, i : i + 1, :]


def conv_kernel(
    heads, state, xr_ref, left_ref, right_ref, w_ref, bias_ref, proj_ref, rv_ref, cv_ref,
    x_ref, rc_ref, cc_ref, f0_ref, f1_ref, f2_ref, f3_ref,
):
    rows_n, cols_n, width = x_ref.shape
    place = lax.broadcasted_iota(jnp.int32, (cols_n, LANES), 0)

    def one_row(r, carry):
        for b in range(width // LANES):
            at = slice(b * LANES, (b + 1) * LANES)
            tap = [0.0, 0.0, 0.0]
            edge = [0.0, 0.0]
            for i in range(3):
                v = xr_ref[r + i, :, at].astype(F32)
                for j in range(3):
                    tap[j] = tap[j] + v * w_ref[3 * i + j : 3 * i + j + 1, at]
                edge[0] = edge[0] + left_ref[r + i, :, at].astype(F32) * w_ref[3 * i : 3 * i + 1, at]
                edge[1] = (
                    edge[1] + right_ref[r + i, :, at].astype(F32) * w_ref[3 * i + 2 : 3 * i + 3, at]
                )
            total = tap[1] + bias_ref[:, at]
            total = total + jnp.where(place == 0, edge[0], pltpu.roll(tap[0], 1, 0))
            total = total + jnp.where(place == cols_n - 1, edge[1], pltpu.roll(tap[2], cols_n - 1, 0))
            x_ref[r, :, at] = silu(total).astype(BF).astype(F32)
        x = x_ref[r].astype(BF)
        coefs = lax.dot_general(
            proj_ref[...], x, (((0,), (1,)), ((), ())), preferred_element_type=F32
        ).astype(BF)
        rc_ref[r] = coefs
        states(
            x, coefs, 0, row_of(rv_ref, r), heads, state, 1, (f0_ref.at[r], f1_ref.at[r])
        )
        return carry

    lax.fori_loop(0, rows_n, one_row, 0)

    def one_group(g, carry):
        x = x_ref[:, pl.ds(pl.multiple_of(g * GROUP, GROUP), GROUP), :]
        x = x.reshape(rows_n * GROUP, width).astype(BF)
        coefs = lax.dot_general(
            proj_ref[...], x, (((0,), (1,)), ((), ())), preferred_element_type=F32
        ).astype(BF)
        cc_ref[g] = coefs
        states(
            x, coefs, 1, row_of(cv_ref, g), heads, state, GROUP, (f2_ref.at[g], f3_ref.at[g])
        )
        return carry

    lax.fori_loop(0, cols_n // GROUP, one_group, 0)


def hop(chain, axis, reverse, k, final_ref, decay_ref, enter_ref, land_ref, send_ref, send_sem, recv_sem):
    count, index = lax.axis_size(axis), lax.axis_index(axis)
    first, last = (count - 1, 0) if reverse else (0, count - 1)
    towards = index - 1 if reverse else index + 1
    lines = final_ref.shape[0]
    each = decay_ref.shape[1]
    state = final_ref.shape[1] // each

    def copy():
        return pltpu.make_async_remote_copy(
            src_ref=send_ref,
            dst_ref=land_ref,
            send_sem=send_sem.at[k],
            recv_sem=recv_sem.at[k],
            device_id={axis: towards},
            device_id_type=pl.DeviceIdType.MESH,
        )

    if chain == "send_done":

        @pl.when(index != last)
        def _():
            copy().wait_send()

        return

    @pl.when(index == first)
    def _():
        def put(i, carry):
            enter_ref[i] = jnp.zeros(enter_ref.shape[1:], BF)
            send_ref[i] = final_ref[i]
            return carry

        lax.fori_loop(0, lines, put, 0)

    @pl.when(index != first)
    def _():
        copy().wait_recv()

        def put(i, carry):
            got = land_ref[i]
            enter_ref[i] = got
            for c in range(each):
                at = slice(c * state, (c + 1) * state)
                passed = decay_ref[i, c : c + 1, :] * got[at].astype(F32) + final_ref[i, at, :].astype(F32)
                send_ref[i, at, :] = passed.astype(BF)
            return carry

        lax.fori_loop(0, lines, put, 0)

    @pl.when(index != last)
    def _():
        copy().start()


def greet(axes):
    barrier = pltpu.get_barrier_semaphore()
    peers = 0
    for axis in axes:
        count, index = lax.axis_size(axis), lax.axis_index(axis)
        for there, step in ((index > 0, -1), (index < count - 1, 1)):

            @pl.when(there)
            def _(axis=axis, step=step, index=index):
                pl.semaphore_signal(
                    barrier,
                    inc=1,
                    device_id={axis: index + step},
                    device_id_type=pl.DeviceIdType.MESH,
                )

            peers = peers + jnp.where(there, 1, 0)
    pl.semaphore_wait(barrier, peers)


def inner_kernel(heads, state, *refs):
    x_ref, rc_ref, cc_ref, rv_ref, cv_ref, ra_ref, ca_ref, skip_ref = refs[:8]
    finals, decays, (y_ref,), enters = refs[8:12], refs[12:16], refs[16:17], refs[17:21]
    lands, sends, (send_sem, recv_sem) = refs[21:25], refs[25:29], refs[29:]
    rows_n, cols_n, width = x_ref.shape
    steps = rows_n + cols_n // GROUP
    ways = (("col", False), ("col", True), ("row", False), ("row", True))

    def pass_on(what, k):
        axis, reverse = ways[k]
        hop(
            what, axis, reverse, k, finals[k], decays[k], enters[k], lands[k], sends[k], send_sem, recv_sem
        )

    def slot(k):
        axis, reverse = ways[k]
        count, index = lax.axis_size(axis), lax.axis_index(axis)
        turn = count - 1 - index if reverse else index
        if axis == "col":
            return turn * max(1, min(6, (steps - 2) // max(1, count - 1)))
        far = max(1, min(24, (steps - 8) // max(1, count // 2 - 1)))
        return turn // 2 * far + turn % 2 * min(6, far)

    greet(("row", "col"))

    def one_row(r):
        x = x_ref[r]
        blocks = inner(x.astype(BF), rc_ref[r], 0, row_of(rv_ref, r), ra_ref[r], heads, state, 1)
        for p, block in enumerate(blocks):
            at = slice(p * LANES, (p + 1) * LANES)
            y_ref[r, :, at] = block + skip_ref[:, at] * x[:, at]

    def one_group(g):
        here = pl.ds(pl.multiple_of(g * GROUP, GROUP), GROUP)
        x = x_ref[:, here, :].reshape(rows_n * GROUP, width).astype(BF)
        blocks = inner(x, cc_ref[g], 1, row_of(cv_ref, g), ca_ref[g], heads, state, GROUP)
        for p, block in enumerate(blocks):
            at = slice(p * LANES, (p + 1) * LANES)
            y_ref[:, here, at] += block.reshape(rows_n, GROUP, LANES)

    def step(s, carry):
        for k in (2, 3, 0, 1):

            @pl.when(s == slot(k))
            def _(k=k):
                pass_on("hop", k)

        @pl.when(s < rows_n)
        def _():
            one_row(s)

        @pl.when(s >= rows_n)
        def _():
            one_group(s - rows_n)

        return carry

    lax.fori_loop(0, steps, step, 0)
    for k in range(4):
        pass_on("send_done", k)


def finish_kernel(
    heads, state, y_ref, rc_ref, cc_ref, rv_ref, cv_ref, e0_ref, e1_ref, e2_ref, e3_ref,
    z_ref, grid_ref, gain_ref, out_w_ref, mlp_gain_ref, ff_in_ref, ff_out_ref, out_ref, sum_ref,
):
    rows_n, cols_n, width = y_ref.shape
    channels = out_ref.shape[2]
    span = 4

    def one_group(g, carry):
        here = pl.ds(pl.multiple_of(g * GROUP, GROUP), GROUP)
        blocks = entered(
            cc_ref[g], 1, row_of(cv_ref, g), heads, state, GROUP, (e2_ref[g], e3_ref[g])
        )
        for p, block in enumerate(blocks):
            at = slice(p * LANES, (p + 1) * LANES)
            sum_ref[:, here, at] = y_ref[:, here, at] + block.reshape(rows_n, GROUP, LANES)
        return carry

    lax.fori_loop(0, cols_n // GROUP, one_group, 0)

    def some_rows(s, carry):
        for i in range(span):
            r = s * span + i
            blocks = entered(rc_ref[r], 0, row_of(rv_ref, r), heads, state, 1, (e0_ref[r], e1_ref[r]))
            for p, block in enumerate(blocks):
                at = slice(p * LANES, (p + 1) * LANES)
                sum_ref[r, :, at] += block
        here = pl.ds(s * span, span)
        cells = span * cols_n
        total = sum_ref[here].reshape(cells, width)
        gate = z_ref[here].reshape(cells, width).astype(F32)
        gated = (rms(total, gain_ref[...]) * silu(gate)).astype(BF)
        held = grid_ref[here].reshape(cells, channels).astype(F32)
        middle = (dot(gated, out_w_ref[...]) + held).astype(BF).astype(F32)
        normed = rms(middle, mlp_gain_ref[...]).astype(BF)
        v = dot(normed, ff_in_ref[...])
        hidden = (v * 0.5 * (1.0 + lax.erf(v * 0.7071067811865476))).astype(BF)
        out = dot(hidden, ff_out_ref[...]) + middle
        out_ref[here] = out.astype(BF).reshape(span, cols_n, channels)
        return carry

    lax.fori_loop(0, rows_n // span, some_rows, 0)


def call(kernel, name, args, out_shape, scratch=(), **params):
    return pl.pallas_call(
        kernel,
        in_specs=[VMEM] * len(args),
        out_specs=[VMEM] * len(out_shape),
        out_shape=out_shape,
        scratch_shapes=list(scratch),
        compiler_params=pltpu.CompilerParams(**PARAMS, **params),
        name=name,
    )(*args)


def rate_vectors(rates, lines, per_head):
    sets, _, heads, length = rates.shape
    i = jnp.arange(length)
    own = (i[:, None] - i[None, :]) % lines == 0
    up = own & (i[:, None] <= i[None, :])
    tri = jnp.stack([up, up.T]).astype(F32)
    high = lax.Precision.HIGHEST
    cum = jnp.einsum("gkht,ktu->gkhu", rates, tri, precision=high)
    ends = jnp.einsum("gkht,tu->gkhu", rates, own.astype(F32), precision=high)
    square = -jnp.expm1(-2.0 * rates)
    weight = jnp.sqrt(square)
    shifted = cum + 0.5 * jnp.log(square)
    to_end = jnp.exp(jnp.minimum(cum - ends, 0.0)) * weight
    from_start = jnp.exp(-cum)
    both = (sets, 2 * heads, length)
    vecs = jnp.concatenate(
        [shifted.reshape(both), weight[:, 1], to_end.reshape(both), from_start.reshape(both)], axis=1
    )
    spread = jnp.repeat(jnp.eye(heads, dtype=F32), per_head, axis=1)
    decay = jnp.einsum("gkhc,hp->kgcp", jnp.exp(-ends[..., :lines]), spread, precision=high)
    return vecs, jnp.swapaxes(cum.reshape(both), 1, 2), decay


def halo(block, axis, dim):
    count = lax.axis_size(axis)
    forward = [(i, i + 1) for i in range(count - 1)]
    backward = [(b, a) for a, b in forward]
    n = block.shape[dim]
    low = lax.ppermute(lax.slice_in_dim(block, n - 1, n, axis=dim), axis, forward)
    high = lax.ppermute(lax.slice_in_dim(block, 0, 1, axis=dim), axis, backward)
    return low, high


def local(
    tile_feats, tile_cell, tile_mask, tile_count, background, norm_gain, in_x, in_z, conv_w,
    conv_bias, x_proj, skip_gain, decay_rate, out_gain, out_w, mlp_gain, ff_in, ff_out,
):
    heads, rows_n, cols_n = decay_rate.shape[1:]
    channels = tile_feats.shape[3]
    slots = tile_feats.shape[2]
    width = in_x.shape[1]
    state = x_proj.shape[1] // 8
    groups = cols_n // GROUP
    cells = rows_n * cols_n

    values = jnp.where(tile_mask[..., None] == 1, tile_feats, background)
    live = jnp.arange(slots, dtype=jnp.int32)[None, None, :] < tile_count[:, :, None]
    marked = jnp.where(live, tile_cell, cells)
    named = jnp.stack([marked // LANES, marked % LANES], axis=-1).astype(BF)
    sent = jnp.concatenate([values, named], axis=-1)
    got = lax.all_to_all(sent, ("row", "col"), split_axis=1, concat_axis=0, tiled=True)

    per_head = width // heads
    rows_first = jnp.transpose(decay_rate[:2], (2, 0, 1, 3))
    rv, ra, rd = rate_vectors(rows_first, 1, per_head)
    cols_first = jnp.transpose(
        decay_rate[2:].reshape(2, heads, rows_n, groups, GROUP), (3, 0, 1, 2, 4)
    ).reshape(groups, 2, heads, rows_n * GROUP)
    cv, ca, cd = rate_vectors(cols_first, GROUP, per_head)
    got, rv, ra, rd, cv, ca, cd = lax.optimization_barrier((got, rv, ra, rd, cv, ca, cd))

    got = got.reshape(-1, channels + 2)
    got_cells = got[:, channels:].astype(jnp.int32)
    got_cells = got_cells[:, 0] * LANES + got_cells[:, 1]
    grid, inner_x, gate = place(
        got_cells.reshape(1, -1),
        got,
        norm_gain[None],
        jnp.concatenate([in_x, in_z], axis=1),
        cells,
    )
    grid = grid.reshape(rows_n, cols_n, channels)
    gate = gate.reshape(rows_n, cols_n, width)
    inner_x = inner_x.reshape(rows_n, cols_n, width)
    top, bottom = halo(inner_x, "row", 0)
    tall = jnp.concatenate([top, inner_x, bottom], axis=0)
    left, right = halo(tall, "col", 1)

    one_row = jax.ShapeDtypeStruct((rows_n, state, width), BF)
    one_col = jax.ShapeDtypeStruct((groups, GROUP * state, width), BF)
    x, rc, cc, f0, f1, f2, f3 = call(
        functools.partial(conv_kernel, heads, state),
        "conv_states",
        (tall, left, right, conv_w.reshape(9, width), conv_bias[None], x_proj, rv, cv),
        [
            jax.ShapeDtypeStruct((rows_n, cols_n, width), F32),
            jax.ShapeDtypeStruct((rows_n, x_proj.shape[1], cols_n), BF),
            jax.ShapeDtypeStruct((groups, x_proj.shape[1], rows_n * GROUP), BF),
            one_row, one_row, one_col, one_col,
        ],
    )

    passed = [one_row, one_row, one_col, one_col]
    slots_of = [pltpu.VMEM(shape.shape, shape.dtype) for shape in passed]
    y, e0, e1, e2, e3 = call(
        functools.partial(inner_kernel, heads, state),
        "inner",
        (x, rc, cc, rv, cv, ra, ca, skip_gain[None], f0, f1, f2, f3, rd[0], rd[1], cd[0], cd[1]),
        [jax.ShapeDtypeStruct((rows_n, cols_n, width), F32)] + passed,
        scratch=slots_of + slots_of + [pltpu.SemaphoreType.DMA((4,)), pltpu.SemaphoreType.DMA((4,))],
        collective_id=0,
        has_side_effects=True,
    )
    return call(
        functools.partial(finish_kernel, heads, state),
        "finish",
        (
            y, rc, cc, rv, cv, e0, e1, e2, e3, gate, grid, out_gain[None], out_w,
            mlp_gain[None], ff_in, ff_out,
        ),
        [jax.ShapeDtypeStruct((rows_n, cols_n, channels), BF)],
        scratch=[pltpu.VMEM((rows_n, cols_n, width), F32)],
    )[0]


def solution(mesh):
    placed = (
        P(("row", "col"), None, None, None),
        P(("row", "col"), None, None),
        P(("row", "col"), None, None),
        P(("row", "col"), None),
        P(), P(), P(), P(), P(), P(), P(), P(),
        P(None, None, "row", "col"),
        P(), P(), P(), P(), P(),
    )
    return jax.shard_map(
        local, mesh=mesh, in_specs=placed, out_specs=P("row", "col", None), check_vma=False
    )
```

```python
import functools

import jax
import jax.numpy as jnp
from jax import lax
from jax.experimental import pallas as pl
from jax.experimental.pallas import tpu as pltpu
from jax.sharding import PartitionSpec as P

BF = jnp.bfloat16
F32 = jnp.float32
VMEM = pl.BlockSpec(memory_space=pltpu.VMEM)
PARAMS = dict(vmem_limit_bytes=56 * 1024 * 1024)
GROUP = 8
LANES = 128
SPAN = 4
PARTS = 4


def dot(a, b):
    return jnp.dot(a, b, preferred_element_type=F32)


def dot_t(a, b):
    return lax.dot_general(a, b, (((0,), (0,)), ((), ())), preferred_element_type=F32)


def silu(v):
    return v / (1.0 + jnp.exp(-v))


def rms(v, gains):
    return v * lax.rsqrt(jnp.mean(v * v, axis=-1, keepdims=True) + 1e-06) * gains


def place_kernel(cells_ref, values_ref, gain_ref, w_ref, grid_ref, x_ref, z_ref):
    tile, channels = grid_ref.shape
    slots = values_ref.shape[0]
    chunk = min(slots, 1024)
    base = pl.program_id(0) * tile
    ids = base + lax.broadcasted_iota(jnp.int32, (tile, chunk), 0)

    def add(k, acc):
        at = pl.ds(pl.multiple_of(k * chunk, chunk), chunk)
        hot = jnp.where(ids == cells_ref[:, at], 1.0, 0.0).astype(BF)
        return acc + dot(hot, values_ref[at, :])

    acc = lax.fori_loop(0, slots // chunk, add, jnp.zeros((tile, values_ref.shape[1]), F32))
    acc = acc[:, :channels]
    grid_ref[...] = acc.astype(BF)
    normed = rms(acc, gain_ref[...]).astype(BF)
    both = dot(normed, w_ref[...]).astype(BF)
    width = x_ref.shape[1]
    x_ref[...] = both[:, :width]
    z_ref[...] = both[:, width:]


def place(cells, values, gain, w, n_cells):
    channels, width = w.shape[0], w.shape[1] // 2
    tile = 512

    def whole(shape):
        return pl.BlockSpec(shape, lambda i: (0, 0))

    def rows(n):
        return pl.BlockSpec((tile, n), lambda i: (i, 0))

    return pl.pallas_call(
        place_kernel,
        grid=(n_cells // tile,),
        in_specs=[whole(cells.shape), whole(values.shape), whole(gain.shape), whole(w.shape)],
        out_specs=[rows(channels), rows(width), rows(width)],
        out_shape=[
            jax.ShapeDtypeStruct((n_cells, channels), BF),
            jax.ShapeDtypeStruct((n_cells, width), BF),
            jax.ShapeDtypeStruct((n_cells, width), BF),
        ],
        compiler_params=pltpu.CompilerParams(**PARAMS),
        name="place",
    )(cells, values, gain, w)


def lane_low(shape):
    return lax.broadcasted_iota(jnp.int32, shape, 1) < LANES // 2


def by_line(coef, lines):
    if lines == 1:
        return coef
    many = jnp.concatenate([coef] * lines, axis=0)
    line = lax.broadcasted_iota(jnp.int32, many.shape, 0) // coef.shape[0]
    own = lax.rem(lax.broadcasted_iota(jnp.int32, many.shape, 1), lines)
    return jnp.where(line == own, many, 0.0)


def coef_of(coefs, index, state):
    return coefs[index * state : (index + 1) * state, :].astype(F32)


def states(x, coefs, pair, vec, heads, state, lines, out_refs):
    for way in range(2):
        spread = by_line(coef_of(coefs, 2 * (2 * pair + way), state), lines)
        n = spread.shape[0]
        for p in range(heads // 2):
            both = jnp.concatenate(
                [spread * vec((3 + way) * heads + 2 * p + i) for i in range(2)], axis=0
            ).astype(BF)
            res = dot(both, x[:, p * LANES : (p + 1) * LANES])
            res = jnp.where(lane_low((n, LANES)), res[:n], res[n:])
            out_refs[way][:, p * LANES : (p + 1) * LANES] = res.astype(BF)


def inner(x, coefs, pair, vec, col, heads, state, lines):
    length = x.shape[0]
    shape = (length, length)
    t = lax.broadcasted_iota(jnp.int32, shape, 0)
    u = lax.broadcasted_iota(jnp.int32, shape, 1)
    ahead = t >= u
    same = t == u
    b0, c0, b1, c1 = (coefs[(4 * pair + i) * state : (4 * pair + i + 1) * state, :] for i in range(4))
    scores = jnp.where(ahead, dot_t(c0, b0), dot_t(c1, b1))
    if lines > 1:
        scores = jnp.where(lax.rem(t, lines) == lax.rem(u, lines), scores, 0.0)
    own = jnp.sum(b1.astype(F32) * c1.astype(F32), axis=0, keepdims=True)
    blocks = []
    for p in range(heads // 2):
        part = []
        for h in (2 * p, 2 * p + 1):
            gap = jnp.where(
                ahead,
                vec(h) - col[:, h : h + 1],
                vec(heads + h) - col[:, heads + h : heads + h + 1],
            )
            mix = jnp.exp(gap) * scores + jnp.where(same, vec(2 * heads + h) * own, 0.0)
            part.append(dot(mix.astype(BF), x[:, p * LANES : (p + 1) * LANES]))
        blocks.append(jnp.where(lane_low((length, LANES)), part[0], part[1]))
    return blocks


def entered(coefs, pair, vec, heads, state, lines, entering):
    spread = [by_line(coef_of(coefs, 2 * (2 * pair + way) + 1, state), lines) for way in range(2)]
    blocks = []
    for p in range(heads // 2):
        left, right = [], []
        for way in range(2):
            held = entering[way][:, p * LANES : (p + 1) * LANES].astype(F32)
            low = lane_low(held.shape)
            left += [spread[way] * vec((5 + way) * heads + 2 * p + i) for i in range(2)]
            right += [jnp.where(low, held, 0.0), jnp.where(low, 0.0, held)]
        blocks.append(
            dot_t(
                jnp.concatenate(left, axis=0).astype(BF), jnp.concatenate(right, axis=0).astype(BF)
            )
        )
    return blocks


def row_of(ref, g):
    return lambda i: ref[g, i : i + 1, :]


def conv_kernel(
    heads, state, xr_ref, left_ref, right_ref, w_ref, bias_ref, proj_ref, rv_ref, cv_ref,
    x_ref, rc_ref, cc_ref, f0_ref, f1_ref, f2_ref, f3_ref,
):
    rows_n, cols_n, width = x_ref.shape
    place = lax.broadcasted_iota(jnp.int32, (cols_n, LANES), 0)

    def one_row(r, carry):
        for b in range(width // LANES):
            at = slice(b * LANES, (b + 1) * LANES)
            tap = [0.0, 0.0, 0.0]
            edge = [0.0, 0.0]
            for i in range(3):
                v = xr_ref[r + i, :, at].astype(F32)
                for j in range(3):
                    tap[j] = tap[j] + v * w_ref[3 * i + j : 3 * i + j + 1, at]
                edge[0] = edge[0] + left_ref[r + i, :, at].astype(F32) * w_ref[3 * i : 3 * i + 1, at]
                edge[1] = (
                    edge[1] + right_ref[r + i, :, at].astype(F32) * w_ref[3 * i + 2 : 3 * i + 3, at]
                )
            total = tap[1] + bias_ref[:, at]
            total = total + jnp.where(place == 0, edge[0], pltpu.roll(tap[0], 1, 0))
            total = total + jnp.where(place == cols_n - 1, edge[1], pltpu.roll(tap[2], cols_n - 1, 0))
            x_ref[r, :, at] = silu(total).astype(BF).astype(F32)
        x = x_ref[r].astype(BF)
        coefs = lax.dot_general(
            proj_ref[...], x, (((0,), (1,)), ((), ())), preferred_element_type=F32
        ).astype(BF)
        rc_ref[r] = coefs
        states(
            x, coefs, 0, row_of(rv_ref, r), heads, state, 1, (f0_ref.at[r], f1_ref.at[r])
        )
        return carry

    lax.fori_loop(0, rows_n, one_row, 0, unroll=2)

    def one_group(g, carry):
        x = x_ref[:, pl.ds(pl.multiple_of(g * GROUP, GROUP), GROUP), :]
        x = x.reshape(rows_n * GROUP, width).astype(BF)
        coefs = lax.dot_general(
            proj_ref[...], x, (((0,), (1,)), ((), ())), preferred_element_type=F32
        ).astype(BF)
        cc_ref[g] = coefs
        states(
            x, coefs, 1, row_of(cv_ref, g), heads, state, GROUP, (f2_ref.at[g], f3_ref.at[g])
        )
        return carry

    lax.fori_loop(0, cols_n // GROUP, one_group, 0, unroll=2)


def hop(what, axis, reverse, k, part, final_ref, decay_ref, enter_ref, land_ref, send_ref, sems):
    count, index = lax.axis_size(axis), lax.axis_index(axis)
    first, last = (count - 1, 0) if reverse else (0, count - 1)
    towards = index - 1 if reverse else index + 1
    lines = final_ref.shape[0] // PARTS
    here = pl.ds(part * lines, lines)
    k = k * PARTS + part
    send_sem, recv_sem = sems
    each = decay_ref.shape[1]
    state = final_ref.shape[1] // each

    def copy():
        return pltpu.make_async_remote_copy(
            src_ref=send_ref.at[here],
            dst_ref=land_ref.at[here],
            send_sem=send_sem.at[k],
            recv_sem=recv_sem.at[k],
            device_id={axis: towards},
            device_id_type=pl.DeviceIdType.MESH,
        )

    if what == "send_done":

        @pl.when(index != last)
        def _():
            copy().wait_send()

        return

    @pl.when(index == first)
    def _():
        def put(i, carry):
            enter_ref[i] = jnp.zeros(enter_ref.shape[1:], BF)
            send_ref[i] = final_ref[i]
            return carry

        lax.fori_loop(part * lines, (part + 1) * lines, put, 0)

    @pl.when(index != first)
    def _():
        copy().wait_recv()

        def put(i, carry):
            got = land_ref[i]
            enter_ref[i] = got
            for c in range(each):
                at = slice(c * state, (c + 1) * state)
                passed = decay_ref[i, c : c + 1, :] * got[at].astype(F32) + final_ref[i, at, :].astype(F32)
                send_ref[i, at, :] = passed.astype(BF)
            return carry

        lax.fori_loop(part * lines, (part + 1) * lines, put, 0)

    @pl.when(index != last)
    def _():
        copy().start()


def greet(axes):
    barrier = pltpu.get_barrier_semaphore()
    peers = 0
    for axis in axes:
        count, index = lax.axis_size(axis), lax.axis_index(axis)
        for there, step in ((index > 0, -1), (index < count - 1, 1)):

            @pl.when(there)
            def _(axis=axis, step=step, index=index):
                pl.semaphore_signal(
                    barrier,
                    inc=1,
                    device_id={axis: index + step},
                    device_id_type=pl.DeviceIdType.MESH,
                )

            peers = peers + jnp.where(there, 1, 0)
    pl.semaphore_wait(barrier, peers)


def inner_kernel(heads, state, *refs):
    x_ref, rc_ref, cc_ref, rv_ref, cv_ref, ra_ref, ca_ref, skip_ref = refs[:8]
    finals, decays, (y_ref,), enters = refs[8:12], refs[12:16], refs[16:17], refs[17:21]
    lands, sends, sems = refs[21:25], refs[25:29], refs[29:]
    rows_n, cols_n, width = x_ref.shape
    row_steps = rows_n // 2
    steps = row_steps + cols_n // GROUP
    ways = (("col", False), ("col", True), ("row", False), ("row", True))

    def pass_on(what, k, part):
        axis, reverse = ways[k]
        hop(
            what, axis, reverse, k, part, finals[k], decays[k], enters[k], lands[k], sends[k], sems
        )

    def slot(k, part):
        axis, reverse = ways[k]
        count, index = lax.axis_size(axis), lax.axis_index(axis)
        turn = count - 1 - index if reverse else index
        apart, each = (2, 3) if axis == "col" else (3, 4)
        each = max(1, min(each, (steps - 1 - (PARTS - 1) * apart) // max(1, count - 1)))
        return turn * each + part * apart

    greet(("row", "col"))

    def two_rows(s):
        done = []
        for r in (2 * s, 2 * s + 1):
            x = x_ref[r]
            blocks = inner(x.astype(BF), rc_ref[r], 0, row_of(rv_ref, r), ra_ref[r], heads, state, 1)
            done.append([
                block + skip_ref[:, p * LANES : (p + 1) * LANES] * x[:, p * LANES : (p + 1) * LANES]
                for p, block in enumerate(blocks)
            ])
        for i in range(2):
            for p, block in enumerate(done[i]):
                y_ref[2 * s + i, :, p * LANES : (p + 1) * LANES] = block

    def one_group(g):
        here = pl.ds(pl.multiple_of(g * GROUP, GROUP), GROUP)
        x = x_ref[:, here, :].reshape(rows_n * GROUP, width).astype(BF)
        blocks = inner(x, cc_ref[g], 1, row_of(cv_ref, g), ca_ref[g], heads, state, GROUP)
        for p, block in enumerate(blocks):
            at = slice(p * LANES, (p + 1) * LANES)
            y_ref[:, here, at] += block.reshape(rows_n, GROUP, LANES)

    def step(s, carry):
        for part in range(PARTS):
            for k in (0, 1, 2, 3):

                @pl.when(s == slot(k, part))
                def _(k=k, part=part):
                    pass_on("hop", k, part)

        @pl.when(s < row_steps)
        def _():
            two_rows(s)

        @pl.when(s >= row_steps)
        def _():
            one_group(s - row_steps)

        return carry

    lax.fori_loop(0, steps, step, 0)
    for k in range(4):
        for part in range(PARTS):
            pass_on("send_done", k, part)


def finish_kernel(
    heads, state, y_ref, rc_ref, cc_ref, rv_ref, cv_ref, e0_ref, e1_ref, e2_ref, e3_ref,
    z_ref, grid_ref, gain_ref, out_w_ref, mlp_gain_ref, ff_in_ref, ff_out_ref, out_ref, sum_ref, held_ref, sem,
):
    rows_n, cols_n, width = y_ref.shape
    channels = out_ref.shape[2]
    span = SPAN

    def leave(s):
        here = pl.ds(s * span, span)
        return pltpu.make_async_copy(held_ref.at[here], out_ref.at[here], sem.at[s])

    def one_group(g, carry):
        here = pl.ds(pl.multiple_of(g * GROUP, GROUP), GROUP)
        blocks = entered(
            cc_ref[g], 1, row_of(cv_ref, g), heads, state, GROUP, (e2_ref[g], e3_ref[g])
        )
        for p, block in enumerate(blocks):
            at = slice(p * LANES, (p + 1) * LANES)
            sum_ref[:, here, at] = y_ref[:, here, at] + block.reshape(rows_n, GROUP, LANES)
        return carry

    lax.fori_loop(0, cols_n // GROUP, one_group, 0)

    def some_rows(s, carry):
        for i in range(span):
            r = s * span + i
            blocks = entered(rc_ref[r], 0, row_of(rv_ref, r), heads, state, 1, (e0_ref[r], e1_ref[r]))
            for p, block in enumerate(blocks):
                at = slice(p * LANES, (p + 1) * LANES)
                sum_ref[r, :, at] += block
        here = pl.ds(s * span, span)
        cells = span * cols_n
        total = sum_ref[here].reshape(cells, width)
        gate = z_ref[here].reshape(cells, width).astype(F32)
        gated = (rms(total, gain_ref[...]) * silu(gate)).astype(BF)
        held = grid_ref[here].reshape(cells, channels).astype(F32)
        middle = (dot(gated, out_w_ref[...]) + held).astype(BF).astype(F32)
        normed = rms(middle, mlp_gain_ref[...]).astype(BF)
        v = dot(normed, ff_in_ref[...])
        hidden = (v * 0.5 * (1.0 + lax.erf(v * 0.7071067811865476))).astype(BF)
        out = dot(hidden, ff_out_ref[...]) + middle
        held_ref[here] = out.astype(BF).reshape(span, cols_n, channels)
        leave(s).start()
        return carry

    lax.fori_loop(0, rows_n // span, some_rows, 0)

    def left(s, carry):
        leave(s).wait()
        return carry

    lax.fori_loop(0, rows_n // span, left, 0)


def call(kernel, name, args, out_shape, scratch=(), out_space=pltpu.VMEM, **params):
    return pl.pallas_call(
        kernel,
        in_specs=[VMEM] * len(args),
        out_specs=[pl.BlockSpec(memory_space=out_space)] * len(out_shape),
        out_shape=out_shape,
        scratch_shapes=list(scratch),
        compiler_params=pltpu.CompilerParams(**PARAMS, **params),
        name=name,
    )(*args)


def rate_vectors(rates, lines, per_head):
    sets, _, heads, length = rates.shape
    i = jnp.arange(length)
    own = (i[:, None] - i[None, :]) % lines == 0
    up = own & (i[:, None] <= i[None, :])
    tri = jnp.stack([up, up.T]).astype(F32)
    high = lax.Precision.HIGHEST
    cum = jnp.einsum("gkht,ktu->gkhu", rates, tri, precision=high)
    ends = jnp.einsum("gkht,tu->gkhu", rates, own.astype(F32), precision=high)
    square = -jnp.expm1(-2.0 * rates)
    weight = jnp.sqrt(square)
    shifted = cum + 0.5 * jnp.log(square)
    to_end = jnp.exp(jnp.minimum(cum - ends, 0.0)) * weight
    from_start = jnp.exp(-cum)
    both = (sets, 2 * heads, length)
    vecs = jnp.concatenate(
        [shifted.reshape(both), weight[:, 1], to_end.reshape(both), from_start.reshape(both)], axis=1
    )
    spread = jnp.repeat(jnp.eye(heads, dtype=F32), per_head, axis=1)
    decay = jnp.einsum("gkhc,hp->kgcp", jnp.exp(-ends[..., :lines]), spread, precision=high)
    return vecs, jnp.swapaxes(cum.reshape(both), 1, 2), decay


def halo(block, axis, dim):
    count = lax.axis_size(axis)
    forward = [(i, i + 1) for i in range(count - 1)]
    backward = [(b, a) for a, b in forward]
    n = block.shape[dim]
    low = lax.ppermute(lax.slice_in_dim(block, n - 1, n, axis=dim), axis, forward)
    high = lax.ppermute(lax.slice_in_dim(block, 0, 1, axis=dim), axis, backward)
    return low, high


def local(
    tile_feats, tile_cell, tile_mask, tile_count, background, norm_gain, in_x, in_z, conv_w,
    conv_bias, x_proj, skip_gain, decay_rate, out_gain, out_w, mlp_gain, ff_in, ff_out,
):
    heads, rows_n, cols_n = decay_rate.shape[1:]
    channels = tile_feats.shape[3]
    slots = tile_feats.shape[2]
    width = in_x.shape[1]
    state = x_proj.shape[1] // 8
    groups = cols_n // GROUP
    cells = rows_n * cols_n

    values = jnp.where(tile_mask[..., None] == 1, tile_feats, background)
    live = jnp.arange(slots, dtype=jnp.int32)[None, None, :] < tile_count[:, :, None]
    marked = jnp.where(live, tile_cell, cells)
    named = jnp.stack([marked // LANES, marked % LANES], axis=-1).astype(BF)
    sent = jnp.concatenate([values, named], axis=-1)
    got = lax.all_to_all(sent, ("row", "col"), split_axis=1, concat_axis=0, tiled=True)

    per_head = width // heads
    rows_first = jnp.transpose(decay_rate[:2], (2, 0, 1, 3))
    rv, ra, rd = rate_vectors(rows_first, 1, per_head)
    cols_first = jnp.transpose(
        decay_rate[2:].reshape(2, heads, rows_n, groups, GROUP), (3, 0, 1, 2, 4)
    ).reshape(groups, 2, heads, rows_n * GROUP)
    cv, ca, cd = rate_vectors(cols_first, GROUP, per_head)
    got, rv, ra, rd, cv, ca, cd = lax.optimization_barrier((got, rv, ra, rd, cv, ca, cd))

    got = got.reshape(-1, channels + 2)
    got_cells = got[:, channels:].astype(jnp.int32)
    got_cells = got_cells[:, 0] * LANES + got_cells[:, 1]
    grid, inner_x, gate = place(
        got_cells.reshape(1, -1),
        got,
        norm_gain[None],
        jnp.concatenate([in_x, in_z], axis=1),
        cells,
    )
    grid = grid.reshape(rows_n, cols_n, channels)
    gate = gate.reshape(rows_n, cols_n, width)
    inner_x = inner_x.reshape(rows_n, cols_n, width)
    top, bottom = halo(inner_x, "row", 0)
    tall = jnp.concatenate([top, inner_x, bottom], axis=0)
    left, right = halo(tall, "col", 1)

    one_row = jax.ShapeDtypeStruct((rows_n, state, width), BF)
    one_col = jax.ShapeDtypeStruct((groups, GROUP * state, width), BF)
    x, rc, cc, f0, f1, f2, f3 = call(
        functools.partial(conv_kernel, heads, state),
        "conv_states",
        (tall, left, right, conv_w.reshape(9, width), conv_bias[None], x_proj, rv, cv),
        [
            jax.ShapeDtypeStruct((rows_n, cols_n, width), F32),
            jax.ShapeDtypeStruct((rows_n, x_proj.shape[1], cols_n), BF),
            jax.ShapeDtypeStruct((groups, x_proj.shape[1], rows_n * GROUP), BF),
            one_row, one_row, one_col, one_col,
        ],
    )

    passed = [one_row, one_row, one_col, one_col]
    slots_of = [pltpu.VMEM(shape.shape, shape.dtype) for shape in passed]
    y, e0, e1, e2, e3 = call(
        functools.partial(inner_kernel, heads, state),
        "inner",
        (x, rc, cc, rv, cv, ra, ca, skip_gain[None], f0, f1, f2, f3, rd[0], rd[1], cd[0], cd[1]),
        [jax.ShapeDtypeStruct((rows_n, cols_n, width), F32)] + passed,
        scratch=slots_of + slots_of + [pltpu.SemaphoreType.DMA((4 * PARTS,))] * 2,
        collective_id=0,
        has_side_effects=True,
    )
    return call(
        functools.partial(finish_kernel, heads, state),
        "finish",
        (
            y, rc, cc, rv, cv, e0, e1, e2, e3, gate, grid, out_gain[None], out_w,
            mlp_gain[None], ff_in, ff_out,
        ),
        [jax.ShapeDtypeStruct((rows_n, cols_n, channels), BF)],
        scratch=[
            pltpu.VMEM((rows_n, cols_n, width), F32),
            pltpu.VMEM((rows_n, cols_n, channels), BF),
            pltpu.SemaphoreType.DMA((rows_n // SPAN,)),
        ],
        out_space=pl.ANY,
    )[0]


def solution(mesh):
    placed = (
        P(("row", "col"), None, None, None),
        P(("row", "col"), None, None),
        P(("row", "col"), None, None),
        P(("row", "col"), None),
        P(), P(), P(), P(), P(), P(), P(), P(),
        P(None, None, "row", "col"),
        P(), P(), P(), P(), P(),
    )
    return jax.shard_map(
        local, mesh=mesh, in_specs=placed, out_specs=P("row", "col", None), check_vma=False
    )
```

```python
import functools

import jax
import jax.numpy as jnp
from jax import lax
from jax.experimental import pallas as pl
from jax.experimental.pallas import tpu as pltpu
from jax.sharding import PartitionSpec as P

BF = jnp.bfloat16
F32 = jnp.float32
VMEM = pl.BlockSpec(memory_space=pltpu.VMEM)
PARAMS = dict(vmem_limit_bytes=56 * 1024 * 1024)
GROUP = 8
LANES = 128
SPAN = 4
PARTS = 4


def dot(a, b):
    return jnp.dot(a, b, preferred_element_type=F32)


def dot_t(a, b):
    return lax.dot_general(a, b, (((0,), (0,)), ((), ())), preferred_element_type=F32)


def silu(v):
    return v / (1.0 + jnp.exp(-v))


def rms(v, gains):
    return v * lax.rsqrt(jnp.mean(v * v, axis=-1, keepdims=True) + 1e-06) * gains


def place_kernel(values_ref, gain_ref, w_ref, grid_ref, x_ref, z_ref):
    tile, channels = grid_ref.shape
    loaders, _, slots = values_ref.shape
    together = 8
    base = pl.program_id(0) * tile
    ids = base + lax.broadcasted_iota(jnp.int32, (tile, together * slots), 0)

    def add(k, acc):
        held = jnp.concatenate([values_ref[k * together + i] for i in range(together)], axis=1)
        named = held[channels:, :].astype(F32)
        cell = (named[0:1] * LANES + named[1:2]).astype(jnp.int32)
        hot = jnp.where(ids == cell, 1.0, 0.0).astype(BF)
        return acc + lax.dot_general(
            hot, held[:channels], (((1,), (1,)), ((), ())), preferred_element_type=F32
        )

    acc = lax.fori_loop(
        0, loaders // together, add, jnp.zeros((tile, channels), F32), unroll=2
    )
    grid_ref[...] = acc.astype(BF)
    normed = rms(acc, gain_ref[...]).astype(BF)
    both = dot(normed, w_ref[...]).astype(BF)
    width = x_ref.shape[1]
    x_ref[...] = both[:, :width]
    z_ref[...] = both[:, width:]


def place(values, gain, w, n_cells):
    channels, width = w.shape[0], w.shape[1] // 2
    tile = 512

    def whole(shape):
        return pl.BlockSpec(shape, lambda i: (0,) * len(shape))

    def rows(n):
        return pl.BlockSpec((tile, n), lambda i: (i, 0))

    return pl.pallas_call(
        place_kernel,
        grid=(n_cells // tile,),
        in_specs=[whole(values.shape), whole(gain.shape), whole(w.shape)],
        out_specs=[rows(channels), rows(width), rows(width)],
        out_shape=[
            jax.ShapeDtypeStruct((n_cells, channels), BF),
            jax.ShapeDtypeStruct((n_cells, width), BF),
            jax.ShapeDtypeStruct((n_cells, width), BF),
        ],
        compiler_params=pltpu.CompilerParams(**PARAMS),
        name="place",
    )(values, gain, w)


def lane_low(shape):
    return lax.broadcasted_iota(jnp.int32, shape, 1) < LANES // 2


def by_line(coef, lines):
    if lines == 1:
        return coef
    many = jnp.concatenate([coef] * lines, axis=0)
    line = lax.broadcasted_iota(jnp.int32, many.shape, 0) // coef.shape[0]
    own = lax.rem(lax.broadcasted_iota(jnp.int32, many.shape, 1), lines)
    return jnp.where(line == own, many, 0.0)


def coef_of(coefs, index, state):
    return coefs[index * state : (index + 1) * state, :].astype(F32)


def states(x, coefs, pair, vec, heads, state, lines, out_refs):
    for way in range(2):
        spread = by_line(coef_of(coefs, 2 * (2 * pair + way), state), lines)
        n = spread.shape[0]
        for p in range(heads // 2):
            both = jnp.concatenate(
                [spread * vec((3 + way) * heads + 2 * p + i) for i in range(2)], axis=0
            ).astype(BF)
            res = dot(both, x[:, p * LANES : (p + 1) * LANES])
            res = jnp.where(lane_low((n, LANES)), res[:n], res[n:])
            out_refs[way][:, p * LANES : (p + 1) * LANES] = res.astype(BF)


def inner(x, coefs, pair, vec, col, heads, state, lines):
    length = x.shape[0]
    shape = (length, length)
    t = lax.broadcasted_iota(jnp.int32, shape, 0)
    u = lax.broadcasted_iota(jnp.int32, shape, 1)
    ahead = t >= u
    same = t == u
    b0, c0, b1, c1 = (coefs[(4 * pair + i) * state : (4 * pair + i + 1) * state, :] for i in range(4))
    scores = jnp.where(ahead, dot_t(c0, b0), dot_t(c1, b1))
    if lines > 1:
        scores = jnp.where(lax.rem(t, lines) == lax.rem(u, lines), scores, 0.0)
    own = jnp.sum(b1.astype(F32) * c1.astype(F32), axis=0, keepdims=True)
    blocks = []
    for p in range(heads // 2):
        part = []
        for h in (2 * p, 2 * p + 1):
            gap = jnp.where(
                ahead,
                vec(h) - col[:, h : h + 1],
                vec(heads + h) - col[:, heads + h : heads + h + 1],
            )
            mix = jnp.exp(gap) * scores + jnp.where(same, vec(2 * heads + h) * own, 0.0)
            part.append(dot(mix.astype(BF), x[:, p * LANES : (p + 1) * LANES]))
        blocks.append(jnp.where(lane_low((length, LANES)), part[0], part[1]))
    return blocks


def entered(coefs, pair, vec, heads, state, lines, entering):
    spread = [by_line(coef_of(coefs, 2 * (2 * pair + way) + 1, state), lines) for way in range(2)]
    blocks = []
    for p in range(heads // 2):
        left, right = [], []
        for way in range(2):
            held = entering[way][:, p * LANES : (p + 1) * LANES].astype(F32)
            low = lane_low(held.shape)
            left += [spread[way] * vec((5 + way) * heads + 2 * p + i) for i in range(2)]
            right += [jnp.where(low, held, 0.0), jnp.where(low, 0.0, held)]
        blocks.append(
            dot_t(
                jnp.concatenate(left, axis=0).astype(BF), jnp.concatenate(right, axis=0).astype(BF)
            )
        )
    return blocks


def row_of(ref, g):
    return lambda i: ref[g, i : i + 1, :]


def conv_rows(
    heads, state, xr_ref, left_ref, right_ref, w_ref, bias_ref, proj_ref, rv_ref,
    x_ref, rc_ref, f0_ref, f1_ref,
):
    rows_n, cols_n, width = x_ref.shape
    place = lax.broadcasted_iota(jnp.int32, (cols_n, LANES), 0)

    def one_row(r, carry):
        for b in range(width // LANES):
            at = slice(b * LANES, (b + 1) * LANES)
            tap = [0.0, 0.0, 0.0]
            edge = [0.0, 0.0]
            for i in range(3):
                v = xr_ref[r + i, :, at].astype(F32)
                for j in range(3):
                    tap[j] = tap[j] + v * w_ref[3 * i + j : 3 * i + j + 1, at]
                edge[0] = edge[0] + left_ref[r + i, :, at].astype(F32) * w_ref[3 * i : 3 * i + 1, at]
                edge[1] = (
                    edge[1] + right_ref[r + i, :, at].astype(F32) * w_ref[3 * i + 2 : 3 * i + 3, at]
                )
            total = tap[1] + bias_ref[:, at]
            total = total + jnp.where(place == 0, edge[0], pltpu.roll(tap[0], 1, 0))
            total = total + jnp.where(place == cols_n - 1, edge[1], pltpu.roll(tap[2], cols_n - 1, 0))
            x_ref[r, :, at] = silu(total).astype(BF).astype(F32)
        x = x_ref[r].astype(BF)
        coefs = lax.dot_general(
            proj_ref[...], x, (((0,), (1,)), ((), ())), preferred_element_type=F32
        ).astype(BF)
        rc_ref[r] = coefs
        states(
            x, coefs, 0, row_of(rv_ref, r), heads, state, 1, (f0_ref.at[r], f1_ref.at[r])
        )
        return carry

    lax.fori_loop(0, rows_n, one_row, 0, unroll=2)


def column_states(heads, state, g, proj_ref, cv_ref, x_ref, cc_ref, f2_ref, f3_ref):
    rows_n, _, width = x_ref.shape
    x = x_ref[:, pl.ds(pl.multiple_of(g * GROUP, GROUP), GROUP), :]
    x = x.reshape(rows_n * GROUP, width).astype(BF)
    coefs = lax.dot_general(
        proj_ref[...], x, (((0,), (1,)), ((), ())), preferred_element_type=F32
    ).astype(BF)
    cc_ref[g] = coefs
    states(x, coefs, 1, row_of(cv_ref, g), heads, state, GROUP, (f2_ref.at[g], f3_ref.at[g]))


def hop(what, axis, reverse, k, part, final_ref, decay_ref, enter_ref, land_ref, send_ref, sems):
    count, index = lax.axis_size(axis), lax.axis_index(axis)
    first, last = (count - 1, 0) if reverse else (0, count - 1)
    towards = index - 1 if reverse else index + 1
    lines = final_ref.shape[0] // PARTS
    here = pl.ds(part * lines, lines)
    k = k * PARTS + part
    send_sem, recv_sem = sems
    each = decay_ref.shape[1]
    state = final_ref.shape[1] // each

    def copy():
        return pltpu.make_async_remote_copy(
            src_ref=send_ref.at[here],
            dst_ref=land_ref.at[here],
            send_sem=send_sem.at[k],
            recv_sem=recv_sem.at[k],
            device_id={axis: towards},
            device_id_type=pl.DeviceIdType.MESH,
        )

    if what == "send_done":

        @pl.when(index != last)
        def _():
            copy().wait_send()

        return

    @pl.when(index == first)
    def _():
        def put(i, carry):
            enter_ref[i] = jnp.zeros(enter_ref.shape[1:], BF)
            send_ref[i] = final_ref[i]
            return carry

        lax.fori_loop(part * lines, (part + 1) * lines, put, 0)

    @pl.when(index != first)
    def _():
        copy().wait_recv()

        def put(i, carry):
            got = land_ref[i]
            enter_ref[i] = got
            for c in range(each):
                at = slice(c * state, (c + 1) * state)
                passed = decay_ref[i, c : c + 1, :] * got[at].astype(F32) + final_ref[i, at, :].astype(F32)
                send_ref[i, at, :] = passed.astype(BF)
            return carry

        lax.fori_loop(part * lines, (part + 1) * lines, put, 0)

    @pl.when(index != last)
    def _():
        copy().start()


def greet(axes):
    barrier = pltpu.get_barrier_semaphore()
    peers = 0
    for axis in axes:
        count, index = lax.axis_size(axis), lax.axis_index(axis)
        for there, step in ((index > 0, -1), (index < count - 1, 1)):

            @pl.when(there)
            def _(axis=axis, step=step, index=index):
                pl.semaphore_signal(
                    barrier,
                    inc=1,
                    device_id={axis: index + step},
                    device_id_type=pl.DeviceIdType.MESH,
                )

            peers = peers + jnp.where(there, 1, 0)
    pl.semaphore_wait(barrier, peers)


def inner_kernel(heads, state, *refs):
    xr_ref, left_ref, right_ref, w_ref, bias_ref, proj_ref, rv_ref, cv_ref, ra_ref, ca_ref, skip_ref = refs[:11]
    decays, (y_ref, rc_ref, cc_ref), enters = refs[11:15], refs[15:18], refs[18:22]
    x_ref, finals, lands, sends, sems = refs[22], refs[23:27], refs[27:31], refs[31:35], refs[35:]
    rows_n, cols_n, width = x_ref.shape
    row_steps = rows_n // 2
    groups = cols_n // GROUP
    state_steps = groups // 2
    steps = state_steps + row_steps + groups
    ways = (("col", False), ("col", True), ("row", False), ("row", True))

    def pass_on(what, k, part):
        axis, reverse = ways[k]
        hop(
            what, axis, reverse, k, part, finals[k], decays[k], enters[k], lands[k], sends[k], sems
        )

    def slot(k, part):
        axis, reverse = ways[k]
        count, index = lax.axis_size(axis), lax.axis_index(axis)
        turn = count - 1 - index if reverse else index
        begin, apart, each = (0, 2, 4) if axis == "col" else (state_steps // PARTS, 3, 4)
        each = max(1, min(each, (steps - 1 - begin - (PARTS - 1) * apart) // max(1, count - 1)))
        return begin + turn * each + part * apart

    greet(("row", "col"))
    conv_rows(
        heads, state, xr_ref, left_ref, right_ref, w_ref, bias_ref, proj_ref, rv_ref,
        x_ref, rc_ref, finals[0], finals[1],
    )

    def two_rows(s):
        done = []
        for r in (2 * s, 2 * s + 1):
            x = x_ref[r]
            blocks = inner(x.astype(BF), rc_ref[r], 0, row_of(rv_ref, r), ra_ref[r], heads, state, 1)
            done.append([
                block + skip_ref[:, p * LANES : (p + 1) * LANES] * x[:, p * LANES : (p + 1) * LANES]
                for p, block in enumerate(blocks)
            ])
        for i in range(2):
            for p, block in enumerate(done[i]):
                y_ref[2 * s + i, :, p * LANES : (p + 1) * LANES] = block

    def one_group(g):
        here = pl.ds(pl.multiple_of(g * GROUP, GROUP), GROUP)
        x = x_ref[:, here, :].reshape(rows_n * GROUP, width).astype(BF)
        blocks = inner(x, cc_ref[g], 1, row_of(cv_ref, g), ca_ref[g], heads, state, GROUP)
        for p, block in enumerate(blocks):
            at = slice(p * LANES, (p + 1) * LANES)
            y_ref[:, here, at] += block.reshape(rows_n, GROUP, LANES)

    def step(s, carry):
        for part in range(PARTS):
            for k in (0, 1, 2, 3):

                @pl.when(s == slot(k, part))
                def _(k=k, part=part):
                    pass_on("hop", k, part)

        @pl.when(s < state_steps)
        def _():
            for i in range(2):
                column_states(
                    heads, state, 2 * s + i, proj_ref, cv_ref, x_ref, cc_ref, finals[2], finals[3]
                )

        @pl.when((s >= state_steps) & (s < state_steps + row_steps))
        def _():
            two_rows(s - state_steps)

        @pl.when(s >= state_steps + row_steps)
        def _():
            one_group(s - state_steps - row_steps)

        return carry

    lax.fori_loop(0, steps, step, 0)
    for k in range(4):
        for part in range(PARTS):
            pass_on("send_done", k, part)


def finish_kernel(
    heads, state, y_ref, rc_ref, cc_ref, rv_ref, cv_ref, e0_ref, e1_ref, e2_ref, e3_ref,
    z_ref, grid_ref, gain_ref, out_w_ref, mlp_gain_ref, ff_in_ref, ff_out_ref, out_ref, sum_ref, held_ref, sem,
):
    rows_n, cols_n, width = y_ref.shape
    channels = out_ref.shape[1]
    span = SPAN

    def leave(s):
        here = pl.ds(s * span, span)
        return pltpu.make_async_copy(held_ref.at[here], out_ref.at[here], sem.at[s])

    def one_group(g, carry):
        here = pl.ds(pl.multiple_of(g * GROUP, GROUP), GROUP)
        blocks = entered(
            cc_ref[g], 1, row_of(cv_ref, g), heads, state, GROUP, (e2_ref[g], e3_ref[g])
        )
        for p, block in enumerate(blocks):
            at = slice(p * LANES, (p + 1) * LANES)
            sum_ref[:, here, at] = y_ref[:, here, at] + block.reshape(rows_n, GROUP, LANES)
        return carry

    lax.fori_loop(0, cols_n // GROUP, one_group, 0)

    def some_rows(s, carry):
        for i in range(span):
            r = s * span + i
            blocks = entered(rc_ref[r], 0, row_of(rv_ref, r), heads, state, 1, (e0_ref[r], e1_ref[r]))
            for p, block in enumerate(blocks):
                at = slice(p * LANES, (p + 1) * LANES)
                sum_ref[r, :, at] += block
        here = pl.ds(s * span, span)
        cells = span * cols_n
        total = sum_ref[here].reshape(cells, width)
        gate = z_ref[here].reshape(cells, width).astype(F32)
        gated = (rms(total, gain_ref[...]) * silu(gate)).astype(BF)
        held = grid_ref[here].reshape(cells, channels).astype(F32)
        middle = (dot(gated, out_w_ref[...]) + held).astype(BF).astype(F32)
        normed = rms(middle, mlp_gain_ref[...]).astype(BF)
        v = dot(normed, ff_in_ref[...])
        hidden = (v * 0.5 * (1.0 + lax.erf(v * 0.7071067811865476))).astype(BF)
        out = dot(hidden, ff_out_ref[...]) + middle
        for i in range(span):
            held_ref[s * span + i] = out[i * cols_n : (i + 1) * cols_n].T.astype(BF)
        leave(s).start()
        return carry

    lax.fori_loop(0, rows_n // span, some_rows, 0)

    def left(s, carry):
        leave(s).wait()
        return carry

    lax.fori_loop(0, rows_n // span, left, 0)


def call(kernel, name, args, out_shape, scratch=(), out_space=pltpu.VMEM, **params):
    return pl.pallas_call(
        kernel,
        in_specs=[VMEM] * len(args),
        out_specs=[pl.BlockSpec(memory_space=out_space)] * len(out_shape),
        out_shape=out_shape,
        scratch_shapes=list(scratch),
        compiler_params=pltpu.CompilerParams(**PARAMS, **params),
        name=name,
    )(*args)


def rate_vectors(rates, lines, per_head):
    sets, _, heads, length = rates.shape
    i = jnp.arange(length)
    own = (i[:, None] - i[None, :]) % lines == 0
    up = own & (i[:, None] <= i[None, :])
    tri = jnp.stack([up, up.T]).astype(F32)
    high = lax.Precision.HIGHEST
    cum = jnp.einsum("gkht,ktu->gkhu", rates, tri, precision=high)
    ends = jnp.einsum("gkht,tu->gkhu", rates, own.astype(F32), precision=high)
    square = -jnp.expm1(-2.0 * rates)
    weight = jnp.sqrt(square)
    shifted = cum + 0.5 * jnp.log(square)
    to_end = jnp.exp(jnp.minimum(cum - ends, 0.0)) * weight
    from_start = jnp.exp(-cum)
    both = (sets, 2 * heads, length)
    vecs = jnp.concatenate(
        [shifted.reshape(both), weight[:, 1], to_end.reshape(both), from_start.reshape(both)], axis=1
    )
    spread = jnp.repeat(jnp.eye(heads, dtype=F32), per_head, axis=1)
    decay = jnp.einsum("gkhc,hp->kgcp", jnp.exp(-ends[..., :lines]), spread, precision=high)
    return vecs, jnp.swapaxes(cum.reshape(both), 1, 2), decay


def halo(block, axis, dim):
    count = lax.axis_size(axis)
    forward = [(i, i + 1) for i in range(count - 1)]
    backward = [(b, a) for a, b in forward]
    n = block.shape[dim]
    low = lax.ppermute(lax.slice_in_dim(block, n - 1, n, axis=dim), axis, forward)
    high = lax.ppermute(lax.slice_in_dim(block, 0, 1, axis=dim), axis, backward)
    return low, high


def local(
    tile_feats, tile_cell, tile_mask, tile_count, background, norm_gain, in_x, in_z, conv_w,
    conv_bias, x_proj, skip_gain, decay_rate, out_gain, out_w, mlp_gain, ff_in, ff_out,
):
    heads, rows_n, cols_n = decay_rate.shape[1:]
    channels = tile_feats.shape[3]
    slots = tile_feats.shape[2]
    width = in_x.shape[1]
    state = x_proj.shape[1] // 8
    groups = cols_n // GROUP
    cells = rows_n * cols_n

    values = jnp.where(tile_mask[..., None] == 1, tile_feats, background)
    live = jnp.arange(slots, dtype=jnp.int32)[None, None, :] < tile_count[:, :, None]
    marked = jnp.where(live, tile_cell, cells)
    named = jnp.stack([marked // LANES, marked % LANES], axis=-1).astype(BF)
    sent = jnp.concatenate([values, named], axis=-1)
    got = lax.all_to_all(sent, ("row", "col"), split_axis=1, concat_axis=0, tiled=True)

    per_head = width // heads
    rows_first = jnp.transpose(decay_rate[:2], (2, 0, 1, 3))
    rv, ra, rd = rate_vectors(rows_first, 1, per_head)
    cols_first = jnp.transpose(
        decay_rate[2:].reshape(2, heads, rows_n, groups, GROUP), (3, 0, 1, 2, 4)
    ).reshape(groups, 2, heads, rows_n * GROUP)
    cv, ca, cd = rate_vectors(cols_first, GROUP, per_head)
    got = jnp.swapaxes(got.reshape(-1, slots, channels + 2), 1, 2)
    got, rv, ra, rd, cv, ca, cd = lax.optimization_barrier((got, rv, ra, rd, cv, ca, cd))

    grid, inner_x, gate = place(
        got, norm_gain[None], jnp.concatenate([in_x, in_z], axis=1), cells
    )
    grid = grid.reshape(rows_n, cols_n, channels)
    gate = gate.reshape(rows_n, cols_n, width)
    inner_x = inner_x.reshape(rows_n, cols_n, width)
    top, bottom = halo(inner_x, "row", 0)
    tall = jnp.concatenate([top, inner_x, bottom], axis=0)
    left, right = halo(tall, "col", 1)

    one_row = jax.ShapeDtypeStruct((rows_n, state, width), BF)
    one_col = jax.ShapeDtypeStruct((groups, GROUP * state, width), BF)
    passed = [one_row, one_row, one_col, one_col]
    slots_of = [pltpu.VMEM(shape.shape, shape.dtype) for shape in passed]
    y, rc, cc, e0, e1, e2, e3 = call(
        functools.partial(inner_kernel, heads, state),
        "conv_scan",
        (
            tall, left, right, conv_w.reshape(9, width), conv_bias[None], x_proj, rv, cv, ra, ca,
            skip_gain[None], rd[0], rd[1], cd[0], cd[1],
        ),
        [
            jax.ShapeDtypeStruct((rows_n, cols_n, width), F32),
            jax.ShapeDtypeStruct((rows_n, x_proj.shape[1], cols_n), BF),
            jax.ShapeDtypeStruct((groups, x_proj.shape[1], rows_n * GROUP), BF),
        ]
        + passed,
        scratch=[pltpu.VMEM((rows_n, cols_n, width), F32)]
        + slots_of * 3
        + [pltpu.SemaphoreType.DMA((4 * PARTS,))] * 2,
        collective_id=0,
        has_side_effects=True,
    )
    out = call(
        functools.partial(finish_kernel, heads, state),
        "finish",
        (
            y, rc, cc, rv, cv, e0, e1, e2, e3, gate, grid, out_gain[None], out_w,
            mlp_gain[None], ff_in, ff_out,
        ),
        [jax.ShapeDtypeStruct((rows_n, channels, cols_n), BF)],
        scratch=[
            pltpu.VMEM((rows_n, cols_n, width), F32),
            pltpu.VMEM((rows_n, channels, cols_n), BF),
            pltpu.SemaphoreType.DMA((rows_n // SPAN,)),
        ],
        out_space=pl.ANY,
    )[0]
    return jnp.swapaxes(out, 1, 2)


def solution(mesh):
    placed = (
        P(("row", "col"), None, None, None),
        P(("row", "col"), None, None),
        P(("row", "col"), None, None),
        P(("row", "col"), None),
        P(), P(), P(), P(), P(), P(), P(), P(),
        P(None, None, "row", "col"),
        P(), P(), P(), P(), P(),
    )
    return jax.shard_map(
        local, mesh=mesh, in_specs=placed, out_specs=P("row", "col", None), check_vma=False
    )
```

```python
import functools

import jax
import jax.numpy as jnp
from jax import lax
from jax.experimental import pallas as pl
from jax.experimental.pallas import tpu as pltpu
from jax.sharding import PartitionSpec as P

BF = jnp.bfloat16
F32 = jnp.float32
VMEM = pl.BlockSpec(memory_space=pltpu.VMEM)
PARAMS = dict(vmem_limit_bytes=56 * 1024 * 1024)
GROUP = 8
LANES = 128
SPAN = 4
PARTS = 4


def dot(a, b):
    return jnp.dot(a, b, preferred_element_type=F32)


def dot_t(a, b):
    return lax.dot_general(a, b, (((0,), (0,)), ((), ())), preferred_element_type=F32)


def silu(v):
    return v / (1.0 + jnp.exp(-v))


def rms(v, gains):
    return v * lax.rsqrt(jnp.mean(v * v, axis=-1, keepdims=True) + 1e-06) * gains


def place_kernel(values_ref, gain_ref, w_ref, grid_ref, x_ref, z_ref):
    tile, channels = grid_ref.shape
    loaders, _, slots = values_ref.shape
    together = 8
    base = pl.program_id(0) * tile
    ids = base + lax.broadcasted_iota(jnp.int32, (tile, together * slots), 0)

    def add(k, acc):
        held = jnp.concatenate([values_ref[k * together + i] for i in range(together)], axis=1)
        named = held[channels:, :].astype(F32)
        cell = (named[0:1] * LANES + named[1:2]).astype(jnp.int32)
        hot = jnp.where(ids == cell, 1.0, 0.0).astype(BF)
        return acc + lax.dot_general(
            hot, held[:channels], (((1,), (1,)), ((), ())), preferred_element_type=F32
        )

    acc = lax.fori_loop(
        0, loaders // together, add, jnp.zeros((tile, channels), F32), unroll=4
    )
    grid_ref[...] = acc.astype(BF)
    normed = rms(acc, gain_ref[...]).astype(BF)
    both = dot(normed, w_ref[...]).astype(BF)
    width = x_ref.shape[1]
    x_ref[...] = both[:, :width]
    z_ref[...] = both[:, width:]


def place(values, gain, w, n_cells):
    channels, width = w.shape[0], w.shape[1] // 2
    tile = 512

    def whole(shape):
        return pl.BlockSpec(shape, lambda i: (0,) * len(shape))

    def rows(n):
        return pl.BlockSpec((tile, n), lambda i: (i, 0))

    return pl.pallas_call(
        place_kernel,
        grid=(n_cells // tile,),
        in_specs=[whole(values.shape), whole(gain.shape), whole(w.shape)],
        out_specs=[rows(channels), rows(width), rows(width)],
        out_shape=[
            jax.ShapeDtypeStruct((n_cells, channels), BF),
            jax.ShapeDtypeStruct((n_cells, width), BF),
            jax.ShapeDtypeStruct((n_cells, width), BF),
        ],
        compiler_params=pltpu.CompilerParams(**PARAMS),
        name="place",
    )(values, gain, w)


def lane_low(shape):
    return lax.broadcasted_iota(jnp.int32, shape, 1) < LANES // 2


def by_line(coef, lines):
    if lines == 1:
        return coef
    many = jnp.concatenate([coef] * lines, axis=0)
    line = lax.broadcasted_iota(jnp.int32, many.shape, 0) // coef.shape[0]
    own = lax.rem(lax.broadcasted_iota(jnp.int32, many.shape, 1), lines)
    return jnp.where(line == own, many, 0.0)


def coef_of(coefs, index, state):
    return coefs[index * state : (index + 1) * state, :].astype(F32)


def states(x, coefs, pair, vec, heads, state, lines, out_refs):
    for way in range(2):
        spread = by_line(coef_of(coefs, 2 * (2 * pair + way), state), lines)
        n = spread.shape[0]
        for p in range(heads // 2):
            both = jnp.concatenate(
                [spread * vec((3 + way) * heads + 2 * p + i) for i in range(2)], axis=0
            ).astype(BF)
            res = dot(both, x[:, p * LANES : (p + 1) * LANES])
            res = jnp.where(lane_low((n, LANES)), res[:n], res[n:])
            out_refs[way][:, p * LANES : (p + 1) * LANES] = res.astype(BF)


def inner(x, coefs, pair, vec, col, heads, state, lines):
    length = x.shape[0]
    shape = (length, length)
    t = lax.broadcasted_iota(jnp.int32, shape, 0)
    u = lax.broadcasted_iota(jnp.int32, shape, 1)
    ahead = t >= u
    same = t == u
    b0, c0, b1, c1 = (coefs[(4 * pair + i) * state : (4 * pair + i + 1) * state, :] for i in range(4))
    scores = jnp.where(ahead, dot_t(c0, b0), dot_t(c1, b1))
    if lines > 1:
        scores = jnp.where(lax.rem(t, lines) == lax.rem(u, lines), scores, 0.0)
    own = jnp.sum(b1.astype(F32) * c1.astype(F32), axis=0, keepdims=True)
    blocks = []
    for p in range(heads // 2):
        part = []
        for h in (2 * p, 2 * p + 1):
            gap = jnp.where(
                ahead,
                vec(h) - col[:, h : h + 1],
                vec(heads + h) - col[:, heads + h : heads + h + 1],
            )
            mix = jnp.exp(gap) * scores + jnp.where(same, vec(2 * heads + h) * own, 0.0)
            part.append(dot(mix.astype(BF), x[:, p * LANES : (p + 1) * LANES]))
        blocks.append(jnp.where(lane_low((length, LANES)), part[0], part[1]))
    return blocks


def entered(coefs, pair, vec, heads, state, lines, entering):
    spread = [by_line(coef_of(coefs, 2 * (2 * pair + way) + 1, state), lines) for way in range(2)]
    blocks = []
    for p in range(heads // 2):
        left, right = [], []
        for way in range(2):
            held = entering[way][:, p * LANES : (p + 1) * LANES].astype(F32)
            low = lane_low(held.shape)
            left += [spread[way] * vec((5 + way) * heads + 2 * p + i) for i in range(2)]
            right += [jnp.where(low, held, 0.0), jnp.where(low, 0.0, held)]
        blocks.append(
            dot_t(
                jnp.concatenate(left, axis=0).astype(BF), jnp.concatenate(right, axis=0).astype(BF)
            )
        )
    return blocks


def row_of(ref, g):
    return lambda i: ref[g, i : i + 1, :]


def conv_rows(
    heads, state, xr_ref, left_ref, right_ref, w_ref, bias_ref, proj_ref, rv_ref,
    x_ref, rc_ref, f0_ref, f1_ref,
):
    rows_n, cols_n, width = x_ref.shape
    place = lax.broadcasted_iota(jnp.int32, (cols_n, LANES), 0)

    def one_row(r, carry):
        for b in range(width // LANES):
            at = slice(b * LANES, (b + 1) * LANES)
            tap = [0.0, 0.0, 0.0]
            edge = [0.0, 0.0]
            for i in range(3):
                v = xr_ref[r + i, :, at].astype(F32)
                for j in range(3):
                    tap[j] = tap[j] + v * w_ref[3 * i + j : 3 * i + j + 1, at]
                edge[0] = edge[0] + left_ref[r + i, :, at].astype(F32) * w_ref[3 * i : 3 * i + 1, at]
                edge[1] = (
                    edge[1] + right_ref[r + i, :, at].astype(F32) * w_ref[3 * i + 2 : 3 * i + 3, at]
                )
            total = tap[1] + bias_ref[:, at]
            total = total + jnp.where(place == 0, edge[0], pltpu.roll(tap[0], 1, 0))
            total = total + jnp.where(place == cols_n - 1, edge[1], pltpu.roll(tap[2], cols_n - 1, 0))
            x_ref[r, :, at] = silu(total).astype(BF).astype(F32)
        x = x_ref[r].astype(BF)
        coefs = lax.dot_general(
            proj_ref[...], x, (((0,), (1,)), ((), ())), preferred_element_type=F32
        ).astype(BF)
        rc_ref[r] = coefs
        states(
            x, coefs, 0, row_of(rv_ref, r), heads, state, 1, (f0_ref.at[r], f1_ref.at[r])
        )
        return carry

    lax.fori_loop(0, rows_n, one_row, 0, unroll=2)


def column_states(heads, state, g, proj_ref, cv_ref, x_ref, cc_ref, f2_ref, f3_ref):
    rows_n, _, width = x_ref.shape
    x = x_ref[:, pl.ds(pl.multiple_of(g * GROUP, GROUP), GROUP), :]
    x = x.reshape(rows_n * GROUP, width).astype(BF)
    coefs = lax.dot_general(
        proj_ref[...], x, (((0,), (1,)), ((), ())), preferred_element_type=F32
    ).astype(BF)
    cc_ref[g] = coefs
    states(x, coefs, 1, row_of(cv_ref, g), heads, state, GROUP, (f2_ref.at[g], f3_ref.at[g]))


def hop(what, axis, reverse, k, part, final_ref, decay_ref, enter_ref, land_ref, send_ref, sems):
    count, index = lax.axis_size(axis), lax.axis_index(axis)
    first, last = (count - 1, 0) if reverse else (0, count - 1)
    towards = index - 1 if reverse else index + 1
    lines = final_ref.shape[0] // PARTS
    here = pl.ds(part * lines, lines)
    k = k * PARTS + part
    send_sem, recv_sem = sems
    each = decay_ref.shape[1]
    state = final_ref.shape[1] // each

    def copy():
        return pltpu.make_async_remote_copy(
            src_ref=send_ref.at[here],
            dst_ref=land_ref.at[here],
            send_sem=send_sem.at[k],
            recv_sem=recv_sem.at[k],
            device_id={axis: towards},
            device_id_type=pl.DeviceIdType.MESH,
        )

    if what == "send_done":

        @pl.when(index != last)
        def _():
            copy().wait_send()

        return

    @pl.when(index == first)
    def _():
        def put(i, carry):
            enter_ref[i] = jnp.zeros(enter_ref.shape[1:], BF)
            send_ref[i] = final_ref[i]
            return carry

        lax.fori_loop(part * lines, (part + 1) * lines, put, 0)

    @pl.when(index != first)
    def _():
        copy().wait_recv()

        def put(i, carry):
            got = land_ref[i]
            enter_ref[i] = got
            for c in range(each):
                at = slice(c * state, (c + 1) * state)
                passed = decay_ref[i, c : c + 1, :] * got[at].astype(F32) + final_ref[i, at, :].astype(F32)
                send_ref[i, at, :] = passed.astype(BF)
            return carry

        lax.fori_loop(part * lines, (part + 1) * lines, put, 0)

    @pl.when(index != last)
    def _():
        copy().start()


def greet(axes):
    barrier = pltpu.get_barrier_semaphore()
    peers = 0
    for axis in axes:
        count, index = lax.axis_size(axis), lax.axis_index(axis)
        for there, step in ((index > 0, -1), (index < count - 1, 1)):

            @pl.when(there)
            def _(axis=axis, step=step, index=index):
                pl.semaphore_signal(
                    barrier,
                    inc=1,
                    device_id={axis: index + step},
                    device_id_type=pl.DeviceIdType.MESH,
                )

            peers = peers + jnp.where(there, 1, 0)
    pl.semaphore_wait(barrier, peers)


def inner_kernel(heads, state, *refs):
    xr_ref, left_ref, right_ref, w_ref, bias_ref, proj_ref, rv_ref, cv_ref, ra_ref, ca_ref, skip_ref = refs[:11]
    decays, (y_ref, rc_ref, cc_ref), enters = refs[11:15], refs[15:18], refs[18:22]
    x_ref, finals, lands, sends, sems = refs[22], refs[23:27], refs[27:31], refs[31:35], refs[35:]
    rows_n, cols_n, width = x_ref.shape
    row_steps = rows_n // 2
    groups = cols_n // GROUP
    state_steps = groups // 2
    steps = state_steps + row_steps + groups
    ways = (("col", False), ("col", True), ("row", False), ("row", True))

    def pass_on(what, k, part):
        axis, reverse = ways[k]
        hop(
            what, axis, reverse, k, part, finals[k], decays[k], enters[k], lands[k], sends[k], sems
        )

    def slot(k, part):
        axis, reverse = ways[k]
        count, index = lax.axis_size(axis), lax.axis_index(axis)
        turn = count - 1 - index if reverse else index
        begin, apart, each = (0, 2, 4) if axis == "col" else (state_steps // PARTS, 3, 4)
        each = max(1, min(each, (steps - 1 - begin - (PARTS - 1) * apart) // max(1, count - 1)))
        return begin + turn * each + part * apart

    greet(("row", "col"))
    conv_rows(
        heads, state, xr_ref, left_ref, right_ref, w_ref, bias_ref, proj_ref, rv_ref,
        x_ref, rc_ref, finals[0], finals[1],
    )

    def two_rows(s):
        done = []
        for r in (2 * s, 2 * s + 1):
            x = x_ref[r]
            blocks = inner(x.astype(BF), rc_ref[r], 0, row_of(rv_ref, r), ra_ref[r], heads, state, 1)
            done.append([
                block + skip_ref[:, p * LANES : (p + 1) * LANES] * x[:, p * LANES : (p + 1) * LANES]
                for p, block in enumerate(blocks)
            ])
        for i in range(2):
            for p, block in enumerate(done[i]):
                y_ref[2 * s + i, :, p * LANES : (p + 1) * LANES] = block

    def one_group(g):
        here = pl.ds(pl.multiple_of(g * GROUP, GROUP), GROUP)
        x = x_ref[:, here, :].reshape(rows_n * GROUP, width).astype(BF)
        blocks = inner(x, cc_ref[g], 1, row_of(cv_ref, g), ca_ref[g], heads, state, GROUP)
        for p, block in enumerate(blocks):
            at = slice(p * LANES, (p + 1) * LANES)
            y_ref[:, here, at] += block.reshape(rows_n, GROUP, LANES)

    def step(s, carry):
        for part in range(PARTS):
            for k in (0, 1, 2, 3):

                @pl.when(s == slot(k, part))
                def _(k=k, part=part):
                    pass_on("hop", k, part)

        @pl.when(s < state_steps)
        def _():
            for i in range(2):
                column_states(
                    heads, state, 2 * s + i, proj_ref, cv_ref, x_ref, cc_ref, finals[2], finals[3]
                )

        @pl.when((s >= state_steps) & (s < state_steps + row_steps))
        def _():
            two_rows(s - state_steps)

        @pl.when(s >= state_steps + row_steps)
        def _():
            one_group(s - state_steps - row_steps)

        return carry

    lax.fori_loop(0, steps, step, 0)
    for k in range(4):
        for part in range(PARTS):
            pass_on("send_done", k, part)


def finish_kernel(
    heads, state, y_ref, rc_ref, cc_ref, rv_ref, cv_ref, e0_ref, e1_ref, e2_ref, e3_ref,
    z_ref, grid_ref, gain_ref, out_w_ref, mlp_gain_ref, ff_in_ref, ff_out_ref, out_ref, sum_ref, held_ref, sem,
):
    rows_n, cols_n, width = y_ref.shape
    channels = out_ref.shape[1]
    span = SPAN

    def leave(s):
        here = pl.ds(s * span, span)
        return pltpu.make_async_copy(held_ref.at[here], out_ref.at[here], sem.at[s])

    def one_group(g, carry):
        here = pl.ds(pl.multiple_of(g * GROUP, GROUP), GROUP)
        blocks = entered(
            cc_ref[g], 1, row_of(cv_ref, g), heads, state, GROUP, (e2_ref[g], e3_ref[g])
        )
        for p, block in enumerate(blocks):
            at = slice(p * LANES, (p + 1) * LANES)
            sum_ref[:, here, at] = y_ref[:, here, at] + block.reshape(rows_n, GROUP, LANES)
        return carry

    lax.fori_loop(0, cols_n // GROUP, one_group, 0, unroll=2)

    def some_rows(s, carry):
        for i in range(span):
            r = s * span + i
            blocks = entered(rc_ref[r], 0, row_of(rv_ref, r), heads, state, 1, (e0_ref[r], e1_ref[r]))
            for p, block in enumerate(blocks):
                at = slice(p * LANES, (p + 1) * LANES)
                sum_ref[r, :, at] += block
        here = pl.ds(s * span, span)
        cells = span * cols_n
        total = sum_ref[here].reshape(cells, width)
        gate = z_ref[here].reshape(cells, width).astype(F32)
        gated = (rms(total, gain_ref[...]) * silu(gate)).astype(BF)
        held = grid_ref[here].reshape(cells, channels).astype(F32)
        middle = (dot(gated, out_w_ref[...]) + held).astype(BF).astype(F32)
        normed = rms(middle, mlp_gain_ref[...]).astype(BF)
        v = dot(normed, ff_in_ref[...])
        hidden = (v * 0.5 * (1.0 + lax.erf(v * 0.7071067811865476))).astype(BF)
        out = dot(hidden, ff_out_ref[...]) + middle
        for i in range(span):
            held_ref[s * span + i] = out[i * cols_n : (i + 1) * cols_n].T.astype(BF)
        leave(s).start()
        return carry

    lax.fori_loop(0, rows_n // span, some_rows, 0)

    def left(s, carry):
        leave(s).wait()
        return carry

    lax.fori_loop(0, rows_n // span, left, 0)


def call(kernel, name, args, out_shape, scratch=(), out_space=pltpu.VMEM, **params):
    return pl.pallas_call(
        kernel,
        in_specs=[VMEM] * len(args),
        out_specs=[pl.BlockSpec(memory_space=out_space)] * len(out_shape),
        out_shape=out_shape,
        scratch_shapes=list(scratch),
        compiler_params=pltpu.CompilerParams(**PARAMS, **params),
        name=name,
    )(*args)


def rate_vectors(rates, lines, per_head):
    sets, _, heads, length = rates.shape
    i = jnp.arange(length)
    own = (i[:, None] - i[None, :]) % lines == 0
    up = own & (i[:, None] <= i[None, :])
    tri = jnp.stack([up, up.T]).astype(F32)
    high = lax.Precision.HIGHEST
    cum = jnp.einsum("gkht,ktu->gkhu", rates, tri, precision=high)
    ends = jnp.einsum("gkht,tu->gkhu", rates, own.astype(F32), precision=high)
    square = -jnp.expm1(-2.0 * rates)
    weight = jnp.sqrt(square)
    shifted = cum + 0.5 * jnp.log(square)
    to_end = jnp.exp(jnp.minimum(cum - ends, 0.0)) * weight
    from_start = jnp.exp(-cum)
    both = (sets, 2 * heads, length)
    vecs = jnp.concatenate(
        [shifted.reshape(both), weight[:, 1], to_end.reshape(both), from_start.reshape(both)], axis=1
    )
    spread = jnp.repeat(jnp.eye(heads, dtype=F32), per_head, axis=1)
    decay = jnp.einsum("gkhc,hp->kgcp", jnp.exp(-ends[..., :lines]), spread, precision=high)
    return vecs, jnp.swapaxes(cum.reshape(both), 1, 2), decay


def halo(block, axis, dim):
    count = lax.axis_size(axis)
    forward = [(i, i + 1) for i in range(count - 1)]
    backward = [(b, a) for a, b in forward]
    n = block.shape[dim]
    low = lax.ppermute(lax.slice_in_dim(block, n - 1, n, axis=dim), axis, forward)
    high = lax.ppermute(lax.slice_in_dim(block, 0, 1, axis=dim), axis, backward)
    return low, high


def local(
    tile_feats, tile_cell, tile_mask, tile_count, background, norm_gain, in_x, in_z, conv_w,
    conv_bias, x_proj, skip_gain, decay_rate, out_gain, out_w, mlp_gain, ff_in, ff_out,
):
    heads, rows_n, cols_n = decay_rate.shape[1:]
    channels = tile_feats.shape[3]
    slots = tile_feats.shape[2]
    width = in_x.shape[1]
    state = x_proj.shape[1] // 8
    groups = cols_n // GROUP
    cells = rows_n * cols_n

    values = jnp.where(tile_mask[..., None] == 1, tile_feats, background)
    live = jnp.arange(slots, dtype=jnp.int32)[None, None, :] < tile_count[:, :, None]
    marked = jnp.where(live, tile_cell, cells)
    named = jnp.stack([marked // LANES, marked % LANES], axis=-1).astype(BF)
    sent = jnp.concatenate([values, named], axis=-1)
    got = lax.all_to_all(sent, ("row", "col"), split_axis=1, concat_axis=0, tiled=True)

    per_head = width // heads
    rows_first = jnp.transpose(decay_rate[:2], (2, 0, 1, 3))
    rv, ra, rd = rate_vectors(rows_first, 1, per_head)
    cols_first = jnp.transpose(
        decay_rate[2:].reshape(2, heads, rows_n, groups, GROUP), (3, 0, 1, 2, 4)
    ).reshape(groups, 2, heads, rows_n * GROUP)
    cv, ca, cd = rate_vectors(cols_first, GROUP, per_head)
    got = jnp.swapaxes(got.reshape(-1, slots, channels + 2), 1, 2)
    got, rv, ra, rd, cv, ca, cd = lax.optimization_barrier((got, rv, ra, rd, cv, ca, cd))

    grid, inner_x, gate = place(
        got, norm_gain[None], jnp.concatenate([in_x, in_z], axis=1), cells
    )
    grid = grid.reshape(rows_n, cols_n, channels)
    gate = gate.reshape(rows_n, cols_n, width)
    inner_x = inner_x.reshape(rows_n, cols_n, width)
    top, bottom = halo(inner_x, "row", 0)
    tall = jnp.concatenate([top, inner_x, bottom], axis=0)
    left, right = halo(tall, "col", 1)

    one_row = jax.ShapeDtypeStruct((rows_n, state, width), BF)
    one_col = jax.ShapeDtypeStruct((groups, GROUP * state, width), BF)
    passed = [one_row, one_row, one_col, one_col]
    slots_of = [pltpu.VMEM(shape.shape, shape.dtype) for shape in passed]
    y, rc, cc, e0, e1, e2, e3 = call(
        functools.partial(inner_kernel, heads, state),
        "conv_scan",
        (
            tall, left, right, conv_w.reshape(9, width), conv_bias[None], x_proj, rv, cv, ra, ca,
            skip_gain[None], rd[0], rd[1], cd[0], cd[1],
        ),
        [
            jax.ShapeDtypeStruct((rows_n, cols_n, width), F32),
            jax.ShapeDtypeStruct((rows_n, x_proj.shape[1], cols_n), BF),
            jax.ShapeDtypeStruct((groups, x_proj.shape[1], rows_n * GROUP), BF),
        ]
        + passed,
        scratch=[pltpu.VMEM((rows_n, cols_n, width), F32)]
        + slots_of * 3
        + [pltpu.SemaphoreType.DMA((4 * PARTS,))] * 2,
        collective_id=0,
        has_side_effects=True,
    )
    out = call(
        functools.partial(finish_kernel, heads, state),
        "finish",
        (
            y, rc, cc, rv, cv, e0, e1, e2, e3, gate, grid, out_gain[None], out_w,
            mlp_gain[None], ff_in, ff_out,
        ),
        [jax.ShapeDtypeStruct((rows_n, channels, cols_n), BF)],
        scratch=[
            pltpu.VMEM((rows_n, cols_n, width), F32),
            pltpu.VMEM((rows_n, channels, cols_n), BF),
            pltpu.SemaphoreType.DMA((rows_n // SPAN,)),
        ],
        out_space=pl.ANY,
    )[0]
    return jnp.swapaxes(out, 1, 2)


def solution(mesh):
    placed = (
        P(("row", "col"), None, None, None),
        P(("row", "col"), None, None),
        P(("row", "col"), None, None),
        P(("row", "col"), None),
        P(), P(), P(), P(), P(), P(), P(), P(),
        P(None, None, "row", "col"),
        P(), P(), P(), P(), P(),
    )
    return jax.shard_map(
        local, mesh=mesh, in_specs=placed, out_specs=P("row", "col", None), check_vma=False
    )
```
